32 devices in a mesh: ctx: 8 (over z, x), tp: 4 (over y, core).
Axes of the slice: x: 2, y: 2, z: 4, core: 2. Of those that a mesh axis runs over, the one named last changes fastest.
Arguments:
- features: bfloat16 [4096, 3, 4096], P(('ctx', 'tp')), may hold values from -6 to 6
- residual: bfloat16 [4096, 4096], P(('ctx', 'tp')), may hold values from -6 to 6
- short_weight: float32 [7, 3, 4096], P(None, None, 'tp'), may hold values from -2 to 2
- rates: float32 [256, 16], P('tp'), may hold values from 0.00012207031 to 0.06
- residues: float32 [256, 16], P('tp'), may hold values from -1.5 to 1.5
- out_weight: bfloat16 [4096, 4096], P('tp'), may hold values from -0.09375 to 0.09375
Outputs:
- mixed: bfloat16 [4096, 4096], P(('ctx', 'tp'))
The draws below stay inside these ranges and needn't reach their ends.
All inputs are finite; a program needn't handle non-finite values.
Results may differ from the reference program's by a relative error of at most 0.023.
Values may be sent and summed in bfloat16 or wider, within the bound.
No kernel may reach another device: no remote copies, remote signals or barrier semaphores. Data moves between devices by JAX's collectives and lax.ppermute only.
A program may use at most 128 MiB of HBM per device.

```python
import math
import jax
import jax.numpy as jnp
from jax import lax

D = 4096
ORDER = 16
GROUP_CH = 16
TOK_CTX = 512
TOKENS = 4096
GROUPS = 256
N_CTX = 8
N_TP = 4


def block_scale(key, dims, split, least, high):
    def one(dim, shards_of):
        steps = jax.random.uniform(jax.random.fold_in(jax.random.fold_in(key, 6), dim), (shards_of,), jnp.float32, least / len(split), high / len(split))
        return jnp.repeat(jnp.exp(steps), dims[dim] // shards_of).reshape((-1,) + (1,) * (len(dims) - dim - 1))

    loudness = one(*split[0])
    for cut in split[1:]:
        loudness = loudness * one(*cut)
    return loudness


def centred(own_key, dims, scale, limit, cuts=(), kind=jnp.bfloat16):
    values = jax.random.normal(own_key, dims, jnp.float32) * scale
    if len(cuts) > 0:
        values = block_scale(own_key, dims, cuts, -0.22, 0.18) * values
    return jnp.clip(values, min=-limit, max=limit).astype(kind)


def setup_inputs(seed: int = 0) -> dict:
    key_list = jax.random.split(jax.random.key(seed), 7)
    features = centred(key_list[0], (TOKENS, 3, D), 1.0, 6.0, ((0, 32),))
    residual = centred(key_list[1], (TOKENS, D), 1.0, 6.0, ((0, 32),))
    short_weight = centred(key_list[2], (7, 3, D), 7 ** -0.5, 2.0, ((2, 4),), jnp.float32)
    rates = jnp.clip(jnp.exp(math.log(0.06) - 6.1975026 * jax.random.uniform(key_list[3], (GROUPS, ORDER), jnp.float32) ** block_scale(key_list[3], (GROUPS, ORDER), ((0, 4),), -0.2, 0.2)), 0.00012207031, 0.06)
    residues = centred(key_list[4], (GROUPS, ORDER), 0.25, 1.5, ((0, 4),), jnp.float32)
    out_weight = centred(key_list[5], (D, D), D ** -0.5, 0.09375, ((0, 4),))
    return {"features": features, "residual": residual, "short_weight": short_weight, "rates": rates, "residues": residues, "out_weight": out_weight}


precise_mode = lax.Precision.HIGHEST

def local_terms(product, rates, coefs):
    block_len = product.shape[0]
    steps_idx = jnp.arange(block_len, dtype=jnp.int32)
    valid = steps_idx[:, None] >= steps_idx[None, :]
    position = steps_idx.astype(jnp.float32)
    falling = coefs[:, :, None] * jnp.exp(-rates[:, :, None] * position)
    rising = jnp.exp(rates[:, :, None] * position)
    matrix = jnp.einsum('gnt,gns->gts', falling, rising, precision=precise_mode)
    matrix = jnp.where(valid[None], matrix, 0.0)
    local = jnp.einsum('gts,sgc->gtc', matrix, product, precision=precise_mode)
    outof = jnp.exp(-rates[:, :, None] * (block_len - 1.0 - position))
    state_here = jnp.einsum('gnt,tgc->ngc', outof, product, precision=precise_mode)
    return (local, state_here)

def carry_terms(rates, coefs, state_in, block_len):
    position = jnp.arange(block_len, dtype=jnp.int32).astype(jnp.float32)
    into = coefs[:, :, None] * jnp.exp(-rates[:, :, None] * (position + 1.0))
    return jnp.einsum('gnt,ngc->gtc', into, state_in, precision=precise_mode)

def long_conv(product, rates, coefs):
    groups = rates.shape[0]
    pieces = product.reshape(N_CTX, TOK_CTX, groups, GROUP_CH)
    decay = jnp.exp(-jnp.transpose(rates) * TOK_CTX)[:, :, None]

    def advance(state, piece):
        local, state_here = local_terms(piece, rates, coefs)
        total = local + carry_terms(rates, coefs, state, TOK_CTX)
        return (decay * state + state_here, jnp.transpose(total, (1, 0, 2)))
    start = jnp.zeros((ORDER, groups, GROUP_CH), jnp.float32)
    unused, outputs = lax.scan(advance, start, pieces)
    return outputs.reshape(N_CTX * TOK_CTX, groups * GROUP_CH)

def reference(features, residual, short_weight, rates, residues, out_weight):
    length = features.shape[0]
    part = D // N_TP
    coefs_all = residues * jnp.sqrt(1.0 - jnp.exp(-2.0 * rates))

    def channel_block(index):
        first = index * part
        block = lax.dynamic_slice_in_dim(features, first, part, 2).astype(jnp.float32)
        taps = lax.dynamic_slice_in_dim(short_weight, first, part, 2)
        padded = jnp.concatenate([jnp.zeros((6, 3, part), jnp.float32), block], 0)
        short = taps[0] * padded[6:]
        for tap_index in range(1, 7):
            short = short + taps[tap_index] * padded[6 - tap_index:6 - tap_index + length]
        query = short[:, 0]
        product = (short[:, 1] * short[:, 2]).reshape(length, part // GROUP_CH, GROUP_CH)
        rate_blk = lax.dynamic_slice_in_dim(rates, index * (part // GROUP_CH), part // GROUP_CH, 0)
        coef_blk = lax.dynamic_slice_in_dim(coefs_all, index * (part // GROUP_CH), part // GROUP_CH, 0)
        longer = long_conv(product, rate_blk, coef_blk)
        return (query * longer).astype(jnp.bfloat16)
    blocks = lax.map(channel_block, jnp.arange(N_TP, dtype=jnp.int32))
    gated = jnp.transpose(blocks, (1, 0, 2)).reshape(length, D)

    def add_part(index, total):
        rows_in = lax.dynamic_slice_in_dim(gated, index * part, part, 1)
        weights = lax.dynamic_slice_in_dim(out_weight, index * part, part, 0)
        term = jnp.dot(rows_in, weights, preferred_element_type=jnp.float32).astype(jnp.bfloat16)
        term = lax.optimization_barrier(term)
        return total + term.astype(jnp.float32)
    summed = lax.fori_loop(0, N_TP, add_part, jnp.zeros((length, D), jnp.float32))
    return (residual.astype(jnp.float32) + summed).astype(jnp.bfloat16)
```

```python
import functools

import jax
import jax.numpy as jnp
from jax import lax
from jax.experimental import pallas as pl
from jax.experimental.pallas import tpu as pltpu
from jax.sharding import PartitionSpec as P

ORDER = 16
GROUP_CH = 16
LANES = 128
TAPS = 7
EDGE = 8
F32 = jnp.float32
BF16 = jnp.bfloat16
PER_TILE = LANES // GROUP_CH


def halves(value):
    high = value.astype(BF16)
    return high, (value - high.astype(F32)).astype(BF16)


def dot(a, b):
    return jnp.dot(a, b, preferred_element_type=F32)


def iota(shape, dim):
    return lax.broadcasted_iota(jnp.int32, shape, dim)


def own_group():
    return iota((LANES, LANES), 0) // ORDER == iota((LANES, LANES), 1) // GROUP_CH


def first_kernel(places, chips, info, feats, taps, rates, residues, kv_out, edge0, edge1, kv_taps, rate_row, coef_row, wide, *rest):
    q_outs, (last, sems) = rest[:places], rest[places:]
    rows, width = q_outs[0].shape
    core, chip = info[0] % 2, info[0] // 2
    copies = []
    for j in range(chips):
        start = pl.multiple_of((2 * j + 1 - core) * width, LANES)
        for branch in range(2):
            copies.append((feats.at[branch + 1, :, pl.ds(start, width)], kv_out.at[branch, :, pl.ds(j * width, width)]))
    copies.append((feats.at[:, pl.ds(rows - 2 * EDGE, 2 * EDGE), :], last))
    for out, (dy, dc) in zip(q_outs, moves(chips)):
        start = pl.multiple_of((2 * ((chip + dy) % chips) + (core + dc) % 2) * width, LANES)
        copies.append((feats.at[0, :, pl.ds(start, width)], out))
    copies = [pltpu.make_async_copy(source, target, sems.at[i]) for i, (source, target) in enumerate(copies)]
    for copy in copies:
        copy.start()

    rate, residue = rates[...], residues[...]
    coef = residue * jnp.sqrt(1.0 - jnp.exp(-2.0 * rate))
    lane_group = iota((ORDER, LANES), 1) // GROUP_CH
    diagonal = iota((ORDER, LANES), 1) % ORDER == iota((ORDER, LANES), 0)

    def spread(values, tile):
        out = jnp.broadcast_to(values[:, tile * PER_TILE : tile * PER_TILE + 1], (ORDER, LANES))
        for g in range(1, PER_TILE):
            at = tile * PER_TILE + g
            out = jnp.where(lane_group == g, jnp.broadcast_to(values[:, at : at + 1], (ORDER, LANES)), out)
        return out

    for b in range(2):
        kv_taps[b, 0:TAPS, :] = taps[b + 1]
    for tile in range(width // LANES):
        lanes = slice(tile * LANES, (tile + 1) * LANES)
        wide_rate = spread(rate, tile)
        wide[:, lanes] = wide_rate
        row = jnp.sum(jnp.where(diagonal, wide_rate, 0.0), axis=0, keepdims=True)
        rate_row[:, lanes] = row
        coef_row[:, lanes] = jnp.sum(jnp.where(diagonal, spread(coef, tile), 0.0), axis=0, keepdims=True)
        for b in range(2):
            kv_taps[b, TAPS : TAPS + 1, lanes] = row
    for copy in copies:
        copy.wait()
    for c, out in ((0, edge0), (1, edge1)):
        for j in range(chips):
            cols = slice((2 * j + c) * width, (2 * j + c + 1) * width)
            for branch in range(3):
                tail = last[branch, :, cols].astype(F32)[EDGE:]
                out[branch, :, j * width : (j + 1) * width] = tail.astype(BF16)


def moves(chips):
    return [(dy, dc) for dy in range(chips) for dc in range(2) if dy or dc]


def first(info, feats, taps, rates, residues, chips):
    _, rows, depth = feats.shape
    width = taps.shape[2]
    places = 2 * chips - 1
    vmem = pl.BlockSpec(memory_space=pltpu.VMEM)
    return pl.pallas_call(
        functools.partial(first_kernel, places, chips),
        out_shape=[
            jax.ShapeDtypeStruct((2, rows, chips * width), BF16),
            jax.ShapeDtypeStruct((3, EDGE, chips * width), BF16),
            jax.ShapeDtypeStruct((3, EDGE, chips * width), BF16),
            jax.ShapeDtypeStruct((2, TAPS + 1, width), F32),
            jax.ShapeDtypeStruct((1, width), F32),
            jax.ShapeDtypeStruct((1, width), F32),
            jax.ShapeDtypeStruct((ORDER, width), F32),
        ]
        + [jax.ShapeDtypeStruct((rows, width), BF16)] * places,
        in_specs=[pl.BlockSpec(memory_space=pltpu.SMEM), pl.BlockSpec(memory_space=pl.ANY), vmem, vmem, vmem],
        out_specs=[vmem] * (7 + places),
        scratch_shapes=[pltpu.VMEM((3, 2 * EDGE, depth), BF16), pltpu.SemaphoreType.DMA((2 * chips + 1 + places,))],
        compiler_params=pltpu.CompilerParams(vmem_limit_bytes=32 << 20),
    )(info, feats, taps, rates, residues)


def fold(product, mask):
    kept = jnp.where(mask, product, 0.0)
    return jnp.sum(kept.reshape(PER_TILE, ORDER, LANES), axis=0)


def convolve(padded, taps, start, count):
    total = taps[0:1] * padded[EDGE + start : EDGE + start + count]
    for j in range(1, TAPS):
        total = total + taps[j : j + 1] * padded[EDGE - j + start : EDGE - j + start + count]
    return total


def front_kernel(chunk, info, k_own, v_own, kv_in, edge0, edge1, taps, near, far, state, pad_k, pad_v, prod):
    rows, width = k_own.shape[1:]
    core = info[0] % 2
    chip_rows = 2 * rows
    chunks = chip_rows // chunk
    mine = pl.multiple_of(EDGE + core * rows, 8)
    other = pl.multiple_of(EDGE + (1 - core) * rows, 8)
    step = min(64, chip_rows)
    mask = own_group()
    age = (chunk - 1 - iota((LANES, chunk), 1)).astype(F32)
    for w in range(width // LANES):
        lanes = slice(w * LANES, (w + 1) * LANES)
        for b, own, pad in ((0, k_own, pad_k), (1, v_own, pad_v)):
            pad[0:EDGE, :] = edge0[b + 1, :, lanes].astype(F32) + edge1[b + 1, :, lanes].astype(F32)
            pad[pl.ds(mine, rows), :] = own[0, :, lanes].astype(F32)
            pad[pl.ds(other, rows), :] = kv_in[b, :, lanes].astype(F32)
        tap_k, tap_v = taps[0, :, lanes], taps[1, :, lanes]
        for start in range(0, chip_rows, step):
            value = convolve(pad_k, tap_k, start, step) * convolve(pad_v, tap_v, start, step)
            prod[start : start + step, :] = value.astype(BF16)
        near[0:rows, lanes] = prod[pl.ds(pl.multiple_of((1 - core) * rows, rows), rows), :]
        far[:, lanes] = prod[pl.ds(pl.multiple_of(core * rows, rows), rows), :]
        rate = jnp.broadcast_to(tap_k[TAPS : TAPS + 1], (LANES, LANES)).T
        high, low = halves(jnp.exp(-rate[:, :chunk] * age))
        beside = jnp.concatenate([prod[i * chunk : (i + 1) * chunk, :] for i in range(chunks)], axis=1)
        reached = dot(high, beside) + dot(low, beside)
        fade = jnp.exp(-rate * float(chunk))
        total = reached[:, :LANES]
        for i in range(1, chunks):
            at = rows + 2 * ORDER * (i - 1)
            inner_high, inner_low = halves(fold(total, mask))
            near[at : at + ORDER, lanes] = inner_high
            near[at + ORDER : at + 2 * ORDER, lanes] = inner_low
            total = fade * total + reached[:, i * LANES : (i + 1) * LANES]
        state[0:ORDER, lanes] = fold(total, mask)
        state[ORDER : ORDER + EDGE, lanes] = edge0[0, :, lanes].astype(F32) + edge1[0, :, lanes].astype(F32)


def front(info, d, chips, feats, kv_in, edge0, edge1, taps, chunk):
    rows = feats.shape[1]
    width = taps.shape[2]
    block = min(512, width)
    per = width // block
    chip_rows = 2 * rows
    stored = rows + 2 * ORDER * (chip_rows // chunk - 1)

    def target(info):
        return (info[0] // 2 + d) % chips

    def own(branch):
        return pl.BlockSpec((1, rows, block), lambda i, info: (branch, 0, (2 * target(info) + info[0] % 2) * per + i))

    return pl.pallas_call(
        functools.partial(front_kernel, chunk),
        grid_spec=pltpu.PrefetchScalarGridSpec(
            num_scalar_prefetch=1,
            grid=(per,),
            in_specs=[
                own(1),
                own(2),
                pl.BlockSpec((2, rows, block), lambda i, info: (0, 0, target(info) * per + i)),
                pl.BlockSpec((3, EDGE, block), lambda i, info: (0, 0, target(info) * per + i)),
                pl.BlockSpec((3, EDGE, block), lambda i, info: (0, 0, target(info) * per + i)),
                pl.BlockSpec((2, TAPS + 1, block), lambda i, info: (0, 0, i)),
            ],
            out_specs=[
                pl.BlockSpec((stored, block), lambda i, info: (0, i)),
                pl.BlockSpec((rows, block), lambda i, info: (0, i)),
                pl.BlockSpec((ORDER + EDGE, block), lambda i, info: (0, i)),
            ],
            scratch_shapes=[pltpu.VMEM((EDGE + chip_rows, LANES), F32)] * 2 + [pltpu.VMEM((chip_rows, LANES), BF16)],
        ),
        out_shape=[
            jax.ShapeDtypeStruct((stored, width), BF16),
            jax.ShapeDtypeStruct((rows, width), BF16),
            jax.ShapeDtypeStruct((ORDER + EDGE, width), F32),
        ],
        compiler_params=pltpu.CompilerParams(vmem_limit_bytes=32 << 20),
    )(info, feats, feats, kv_in, edge0, edge1, taps)


def query_kernel(chips, info, own, *rest):
    places = 2 * chips - 1
    pieces, (edge, taps, out, pad) = rest[:places], rest[places:]
    rows, width = own.shape[1:]
    total_rows = out.shape[0]
    step = min(64, total_rows)
    core, chip = info[0] % 2, info[0] // 2
    for w in range(width // LANES):
        lanes = slice(w * LANES, (w + 1) * LANES)
        pad[0:EDGE, :] = edge[:, lanes]
        pad[pl.ds(pl.multiple_of(EDGE + info[0] * rows, 8), rows), :] = own[0, :, lanes].astype(F32)
        for piece, (dy, dc) in zip(pieces, moves(chips)):
            source = 2 * ((chip + chips - dy) % chips) + (core + dc) % 2
            pad[pl.ds(pl.multiple_of(EDGE + source * rows, 8), rows), :] = piece[:, lanes].astype(F32)
        tap = taps[0, :, lanes]
        for start in range(0, total_rows, step):
            out[start : start + step, lanes] = convolve(pad, tap, start, step)


def query(info, chips, feats, pieces, edge, taps):
    rows, width = pieces[0].shape
    places = len(pieces)
    block = min(512, width)
    per = width // block
    total_rows = rows * (places + 1)
    return pl.pallas_call(
        functools.partial(query_kernel, chips),
        grid_spec=pltpu.PrefetchScalarGridSpec(
            num_scalar_prefetch=1,
            grid=(per,),
            in_specs=[pl.BlockSpec((1, rows, block), lambda i, info: (0, 0, info[0] * per + i))]
            + [pl.BlockSpec((rows, block), lambda i, info: (0, i))] * places
            + [
                pl.BlockSpec((EDGE, block), lambda i, info: (0, i)),
                pl.BlockSpec((1, TAPS, block), lambda i, info: (0, 0, i)),
            ],
            out_specs=pl.BlockSpec((total_rows, block), lambda i, info: (0, i)),
            scratch_shapes=[pltpu.VMEM((EDGE + total_rows, LANES), F32)],
        ),
        out_shape=jax.ShapeDtypeStruct((total_rows, width), F32),
        compiler_params=pltpu.CompilerParams(vmem_limit_bytes=32 << 20),
    )(info, feats, *pieces, edge, taps)


def toeplitz_kernel(chunk, rate_row, coef_row, out):
    lag = (LANES - 1 - iota((LANES, LANES), 1)).astype(F32)
    rate = jnp.broadcast_to(rate_row[...], (LANES, LANES)).T
    coef = jnp.broadcast_to(coef_row[...], (LANES, LANES)).T
    taps = jnp.sum((coef * jnp.exp(-rate * lag)).reshape(PER_TILE, ORDER, LANES), axis=1)
    valid = iota((LANES, LANES), 1) <= iota((LANES, LANES), 0)
    for g in range(PER_TILE):
        spread = jnp.broadcast_to(taps[g : g + 1], (LANES, LANES))
        block = jnp.where(valid, pltpu.roll(spread, 1, 1, stride=1, stride_axis=0), 0.0)
        out[g * chunk : (g + 1) * chunk, :] = block[:chunk, :chunk].astype(BF16)


def toeplitz(rate_row, coef_row, chunk):
    tiles = rate_row.shape[1] // LANES
    return pl.pallas_call(
        functools.partial(toeplitz_kernel, chunk),
        grid=(tiles,),
        in_specs=[pl.BlockSpec((1, LANES), lambda i: (0, i))] * 2,
        out_specs=pl.BlockSpec((PER_TILE * chunk, chunk), lambda i: (i, 0)),
        out_shape=jax.ShapeDtypeStruct((tiles * PER_TILE * chunk, chunk), BF16),
    )(rate_row, coef_row)


def gate_kernel(chunk, theirs, info, prod, inner, toep, q, start_state, wide_rates, rate_row, coef_row, out):
    rows, width = q.shape
    chunks = rows // chunk
    core = info[0] % 2
    half = 1 - core if theirs else core
    mask = own_group()
    lane_group = iota((chunk, LANES), 1) // GROUP_CH
    later = (iota((chunk, LANES), 0) + 1).astype(F32)
    for w in range(width // LANES):
        lanes = slice(w * LANES, (w + 1) * LANES)
        beside = jnp.concatenate([prod[i * chunk : (i + 1) * chunk, lanes] for i in range(chunks)], axis=1)
        blocks = toep[w * PER_TILE * chunk : (w + 1) * PER_TILE * chunk, :]
        local = dot(blocks, beside)
        into_high, into_low = halves(coef_row[:, lanes] * jnp.exp(-rate_row[:, lanes] * later))
        entering = []
        for i in range(chunks):
            place = half * chunks + i
            at = pl.multiple_of(rows + 2 * ORDER * jnp.maximum(place - 1, 0), ORDER)
            kept = inner[pl.ds(at, ORDER), lanes].astype(F32) + inner[pl.ds(at + ORDER, ORDER), lanes].astype(F32)
            state = jnp.exp(-wide_rates[:, lanes] * (place * chunk).astype(F32)) * start_state[:, lanes]
            state = state + jnp.where(place > 0, kept, 0.0)
            entering.append(jnp.where(mask, jnp.concatenate([state] * PER_TILE, axis=0), 0.0))
        state_high, state_low = halves(jnp.concatenate(entering, axis=1))
        carried = dot(into_high, state_high) + dot(into_high, state_low) + dot(into_low, state_high)
        for i in range(chunks):
            cols = slice(i * LANES, (i + 1) * LANES)
            kept = local[:chunk, cols]
            for g in range(1, PER_TILE):
                kept = jnp.where(lane_group == g, local[g * chunk : (g + 1) * chunk, cols], kept)
            gated = q[i * chunk : (i + 1) * chunk, lanes] * (kept + carried[:, cols])
            out[i * chunk : (i + 1) * chunk, lanes] = gated.astype(BF16)


def gate(info, d, chips, theirs, prod, inner, toep, q, start_state, wide_rates, rate_row, coef_row, chunk):
    rows = q.shape[0] // (2 * chips)
    width = q.shape[1]
    block = min(512, width)

    def place(info):
        core = info[0] % 2
        return 2 * ((info[0] // 2 + chips - d) % chips) + (1 - core if theirs else core)

    return pl.pallas_call(
        functools.partial(gate_kernel, chunk, theirs),
        grid_spec=pltpu.PrefetchScalarGridSpec(
            num_scalar_prefetch=1,
            grid=(width // block,),
            in_specs=[
                pl.BlockSpec((rows, block), lambda i, info: (0, i)),
                pl.BlockSpec((inner.shape[0], block), lambda i, info: (0, i)),
                pl.BlockSpec((block // GROUP_CH * chunk, chunk), lambda i, info: (i, 0)),
                pl.BlockSpec((rows, block), lambda i, info: (place(info), i)),
                pl.BlockSpec((ORDER, block), lambda i, info: (0, i)),
                pl.BlockSpec((ORDER, block), lambda i, info: (0, i)),
                pl.BlockSpec((1, block), lambda i, info: (0, i)),
                pl.BlockSpec((1, block), lambda i, info: (0, i)),
            ],
            out_specs=pl.BlockSpec((rows, block), lambda i, info: (0, i)),
        ),
        out_shape=jax.ShapeDtypeStruct((rows, width), BF16),
        compiler_params=pltpu.CompilerParams(vmem_limit_bytes=32 << 20),
    )(info, prod, inner, toep, q, start_state, wide_rates, rate_row, coef_row)


def body(chips, contexts, features, residual, short_weight, rates, residues, out_weight):
    rows, _, depth = features.shape
    chip_rows = 2 * rows
    context_rows = chips * chip_rows
    chunk = min(LANES, rows)
    tp, ctx = lax.axis_index("tp"), lax.axis_index("ctx")
    chip = tp // 2
    info = tp.astype(jnp.int32).reshape(1)

    def along_y(value, by):
        return lax.ppermute(value, "tp", [(i, (i + 2 * by) % (2 * chips)) for i in range(2 * chips)])

    def across(value):
        return lax.ppermute(value, "tp", [(i, i ^ 1) for i in range(2 * chips)])

    def with_context(value, bit):
        return lax.ppermute(value, "ctx", [(i, i ^ bit) for i in range(contexts)])

    feats = jnp.transpose(features, (1, 0, 2))
    taps = jnp.transpose(short_weight, (1, 0, 2))
    sent = first(info, feats, taps, jnp.transpose(rates), jnp.transpose(residues), chips)
    kv_out, edge0, edge1, kv_taps, rate_row, coef_row, wide_rates = sent[:7]

    kv_taps = [kv_taps] + [along_y(kv_taps, -d) for d in range(1, chips)]

    order = [(x, y) for x in range(contexts) for y in range(chips)]
    edges = []
    for c, part in ((0, edge0), (1, edge1)):
        pairs = [
            ((x * chips + y) * 2 + 1, (nx * chips + ny) * 2 + c) for (x, y), (nx, ny) in zip(order[:-1], order[1:])
        ]
        edges.append(lax.ppermute(part, ("ctx", "tp"), pairs))

    kv_in = across(kv_out)
    pieces = []
    for (dy, dc), part in zip(moves(chips), sent[7:]):
        pairs = [(2 * y + c, 2 * ((y + dy) % chips) + (c + dc) % 2) for y in range(chips) for c in range(2)]
        pieces.append(lax.ppermute(part, "tp", pairs))

    nears, fars, states = [None] * chips, [None] * chips, [None] * chips
    for d in list(range(1, chips)) + [0]:
        near, far, state = front(info, d, chips, feats, kv_in, edges[0], edges[1], kv_taps[d], chunk)
        if d > 0:
            state = along_y(state, d)
            near = along_y(near, d)
            far = along_y(far, d)
        nears[d], fars[d], states[d] = near, far, state

    toep_rates, _ = lax.optimization_barrier((rate_row, states[0]))
    toep = toeplitz(toep_rates, coef_row, chunk)

    def of_chip(values, y):
        return sum(jnp.where((chip - d) % chips == y, value, 0.0) for d, value in enumerate(values))

    by_chip = [of_chip(states, y) for y in range(chips)]
    chip_fade = jnp.exp(-wide_rates * float(chip_rows))
    total = by_chip[0][:ORDER]
    for y in range(1, chips):
        total = chip_fade * total + by_chip[y][:ORDER]

    before = jnp.zeros_like(total)
    bit = 1
    while bit < contexts:
        got = with_context(total, bit)
        upper = (ctx & bit) != 0
        place = (ctx & (bit - 1)).astype(F32)
        before = before + jnp.where(upper, jnp.exp(-wide_rates * (place * context_rows)) * got, 0.0)
        fade = jnp.exp(-wide_rates * float(bit * context_rows))
        total = jnp.where(upper, fade * got + total, fade * total + got)
        bit *= 2
    entering = [before]
    for y in range(chips - 1):
        entering.append(chip_fade * entering[-1] + by_chip[y][:ORDER])

    q = query(info, chips, feats, pieces, by_chip[0][ORDER:], taps)

    parts = 2
    cols = depth // parts
    sums = [residual[:, p * cols : (p + 1) * cols].astype(F32) for p in range(parts)]
    for d in list(range(1, chips)) + [0]:
        y = (chip - d) % chips
        start_state = sum(jnp.where(y == i, value, 0.0) for i, value in enumerate(entering))
        gated = [
            gate(info, d, chips, theirs, prod, nears[d], toep, q, start_state, wide_rates, rate_row, coef_row, chunk)
            for theirs, prod in ((True, nears[d]), (False, fars[d]))
        ]
        for p in range(parts):
            weights = out_weight[:, p * cols : (p + 1) * cols]
            theirs = across(dot(gated[0], weights).astype(BF16))
            mine = dot(gated[1], weights) + theirs.astype(F32)
            if d > 0:
                mine = along_y(mine.astype(BF16), -d).astype(F32)
            sums[p] = sums[p] + mine
    return jnp.concatenate([value.astype(BF16) for value in sums], axis=1)


def solution(mesh):
    chips, contexts = mesh.shape["tp"] // 2, mesh.shape["ctx"]
    in_specs = (
        P(("ctx", "tp"), None, None),
        P(("ctx", "tp"), None),
        P(None, None, "tp"),
        P("tp", None),
        P("tp", None),
        P("tp", None),
    )
    return jax.shard_map(
        functools.partial(body, chips, contexts),
        mesh=mesh,
        in_specs=in_specs,
        out_specs=P(("ctx", "tp"), None),
        check_vma=False,
    )
```

```python
import functools

import jax
import jax.numpy as jnp
from jax import lax
from jax.experimental import pallas as pl
from jax.experimental.pallas import tpu as pltpu
from jax.sharding import PartitionSpec as P

ORDER = 16
GROUP_CH = 16
LANES = 128
TAPS = 7
EDGE = 8
F32 = jnp.float32
BF16 = jnp.bfloat16
PER_TILE = LANES // GROUP_CH
BRIEF = pl.CostEstimate(flops=1, bytes_accessed=1, transcendentals=0)


def halves(value):
    high = value.astype(BF16)
    return high, (value - high.astype(F32)).astype(BF16)


def dot(a, b):
    return jnp.dot(a, b, preferred_element_type=F32)


def iota(shape, dim):
    return lax.broadcasted_iota(jnp.int32, shape, dim)


def own_group():
    return iota((LANES, LANES), 0) // ORDER == iota((LANES, LANES), 1) // GROUP_CH


def target(position, e, chips):
    return 2 * ((position // 2 + e // 2) % chips) + (position % 2 + e % 2) % 2


def source(position, e, chips):
    return 2 * ((position // 2 + chips - e // 2) % chips) + (position % 2 + e % 2) % 2


def fold(product, mask):
    kept = jnp.where(mask, product, 0.0)
    return jnp.sum(kept.reshape(PER_TILE, ORDER, LANES), axis=0)


def convolve(padded, taps, start, count):
    total = taps[0:1] * padded[EDGE + start : EDGE + start + count]
    for j in range(1, TAPS):
        total = total + taps[j : j + 1] * padded[EDGE - j + start : EDGE - j + start + count]
    return total


def first_kernel(chips, info, feats, taps_in, rates_in, residues_in, kv_out, edge0, edge1, kv_taps, rate_row, coef_row, wide, *rest):
    steps = 2 * chips
    pieces, (last, taps, rates, residues, sems) = rest[: steps - 1], rest[steps - 1 :]
    rows, width = pieces[0].shape
    core = info[0] % 2
    copies = [(rates_in, rates), (residues_in, residues), (taps_in, taps), (feats.at[:, pl.ds(rows - 2 * EDGE, 2 * EDGE), :], last)]
    for j in range(chips):
        start = pl.multiple_of((2 * j + 1 - core) * width, LANES)
        for branch in range(2):
            copies.append((feats.at[branch + 1, :, pl.ds(start, width)], kv_out.at[branch, :, pl.ds(j * width, width)]))
    for e, piece in enumerate(pieces, 1):
        start = pl.multiple_of(target(info[0], e, chips) * width, LANES)
        copies.append((feats.at[0, :, pl.ds(start, width)], piece))
    copies = [pltpu.make_async_copy(*ends, sems.at[i]) for i, ends in enumerate(copies)]
    for copy in copies:
        copy.start()
    for copy in copies[:3]:
        copy.wait()

    rate, residue = rates[...], residues[...]
    coef = residue * jnp.sqrt(1.0 - jnp.exp(-2.0 * rate))
    lane_group = iota((ORDER, LANES), 1) // GROUP_CH
    diagonal = iota((ORDER, LANES), 1) % ORDER == iota((ORDER, LANES), 0)

    def spread(values, tile):
        out = jnp.broadcast_to(values[:, tile * PER_TILE : tile * PER_TILE + 1], (ORDER, LANES))
        for g in range(1, PER_TILE):
            at = tile * PER_TILE + g
            out = jnp.where(lane_group == g, jnp.broadcast_to(values[:, at : at + 1], (ORDER, LANES)), out)
        return out

    for b in range(2):
        kv_taps[b, 0:TAPS, :] = taps[b + 1]
    for tile in range(width // LANES):
        lanes = slice(tile * LANES, (tile + 1) * LANES)
        wide_rate = spread(rate, tile)
        wide[:, lanes] = wide_rate
        row = jnp.sum(jnp.where(diagonal, wide_rate, 0.0), axis=0, keepdims=True)
        rate_row[:, lanes] = row
        coef_row[:, lanes] = jnp.sum(jnp.where(diagonal, spread(coef, tile), 0.0), axis=0, keepdims=True)
        for b in range(2):
            kv_taps[b, TAPS : TAPS + 1, lanes] = row
    for copy in copies[3:]:
        copy.wait()
    for c, out in ((0, edge0), (1, edge1)):
        for j in range(chips):
            cols = slice((2 * j + c) * width, (2 * j + c + 1) * width)
            for branch in range(3):
                out[branch, :, j * width : (j + 1) * width] = last[branch, :, cols].astype(F32)[EDGE:].astype(BF16)


def first(info, feats, taps, rates, residues, chips):
    _, rows, depth = feats.shape
    width = taps.shape[2]
    others = 2 * chips - 1
    vmem = pl.BlockSpec(memory_space=pltpu.VMEM)
    return pl.pallas_call(
        functools.partial(first_kernel, chips),
        out_shape=[
            jax.ShapeDtypeStruct((2, rows, chips * width), BF16),
            jax.ShapeDtypeStruct((3, EDGE, chips * width), BF16),
            jax.ShapeDtypeStruct((3, EDGE, chips * width), BF16),
            jax.ShapeDtypeStruct((2, TAPS + 1, width), F32),
            jax.ShapeDtypeStruct((1, width), F32),
            jax.ShapeDtypeStruct((1, width), F32),
            jax.ShapeDtypeStruct((ORDER, width), F32),
        ]
        + [jax.ShapeDtypeStruct((rows, width), BF16)] * others,
        in_specs=[pl.BlockSpec(memory_space=pltpu.SMEM)] + [pl.BlockSpec(memory_space=pltpu.HBM)] * 4,
        out_specs=[vmem] * (7 + others),
        scratch_shapes=[
            pltpu.VMEM((3, 2 * EDGE, depth), BF16),
            pltpu.VMEM(taps.shape, F32),
            pltpu.VMEM(rates.shape, F32),
            pltpu.VMEM(residues.shape, F32),
            pltpu.SemaphoreType.DMA((4 + 2 * chips + others,)),
        ],
        compiler_params=pltpu.CompilerParams(vmem_limit_bytes=12 << 20),
        cost_estimate=BRIEF,
    )(info, feats, taps, rates, residues)


def front_kernel(info, k_own, v_own, kv_in, edge0, edge1, taps, prod, state, pad_k, pad_v):
    rows, width = k_own.shape[1:]
    core = info[0] % 2
    chip_rows = 2 * rows
    mine = pl.multiple_of(EDGE + core * rows, 8)
    other = pl.multiple_of(EDGE + (1 - core) * rows, 8)
    step = min(64, chip_rows)
    mask = own_group()
    age = (rows - 1 - iota((LANES, rows), 1)).astype(F32)
    for w in range(width // LANES):
        lanes = slice(w * LANES, (w + 1) * LANES)
        for b, own, pad in ((0, k_own, pad_k), (1, v_own, pad_v)):
            pad[w, 0:EDGE, :] = edge0[b + 1, :, lanes].astype(F32) + edge1[b + 1, :, lanes].astype(F32)
            pad[w, pl.ds(mine, rows), :] = own[0, :, lanes].astype(F32)
            pad[w, pl.ds(other, rows), :] = kv_in[b, :, lanes].astype(F32)
        tap_k, tap_v = taps[0, :, lanes], taps[1, :, lanes]
        for start in range(0, chip_rows, step):
            value = convolve(pad_k.at[w], tap_k, start, step) * convolve(pad_v.at[w], tap_v, start, step)
            prod[start : start + step, lanes] = value.astype(BF16)
        rate = jnp.broadcast_to(tap_k[TAPS : TAPS + 1], (LANES, LANES)).T
        high, low = halves(jnp.exp(-rate[:, :rows] * age))
        beside = jnp.concatenate([prod[0:rows, lanes], prod[rows:chip_rows, lanes]], axis=1)
        reached = dot(jnp.concatenate([high, low], axis=0), beside)
        reached = reached[:LANES] + reached[LANES:]
        inner_high, inner_low = halves(fold(reached[:, :LANES], mask))
        prod[chip_rows : chip_rows + ORDER, lanes] = inner_high
        prod[chip_rows + ORDER : chip_rows + 2 * ORDER, lanes] = inner_low
        state[0:ORDER, lanes] = fold(jnp.exp(-rate * float(rows)) * reached[:, :LANES] + reached[:, LANES:], mask)
        state[ORDER : ORDER + EDGE, lanes] = edge0[0, :, lanes].astype(F32) + edge1[0, :, lanes].astype(F32)


def front(info, d, chips, feats, kv_in, edge0, edge1, taps):
    rows = feats.shape[1]
    width = taps.shape[2]
    block = min(512, width)
    per = width // block
    stored = 2 * rows + 2 * ORDER

    def chip(info):
        return (info[0] // 2 + d) % chips

    def own(branch):
        return pl.BlockSpec((1, rows, block), lambda i, info: (branch, 0, (2 * chip(info) + info[0] % 2) * per + i))

    def of_chip(*shape):
        return pl.BlockSpec(shape + (block,), lambda i, info: (0,) * len(shape) + (chip(info) * per + i,))

    def spec(*shape):
        return pl.BlockSpec(shape + (block,), lambda i, info: (0,) * len(shape) + (i,))

    return pl.pallas_call(
        front_kernel,
        grid_spec=pltpu.PrefetchScalarGridSpec(
            num_scalar_prefetch=1,
            grid=(per,),
            in_specs=[own(1), own(2), of_chip(2, rows), of_chip(3, EDGE), of_chip(3, EDGE), spec(2, TAPS + 1)],
            out_specs=[spec(stored), spec(ORDER + EDGE)],
            scratch_shapes=[pltpu.VMEM((block // LANES, EDGE + 2 * rows, LANES), F32)] * 2,
        ),
        out_shape=[jax.ShapeDtypeStruct((stored, width), BF16), jax.ShapeDtypeStruct((ORDER + EDGE, width), F32)],
        compiler_params=pltpu.CompilerParams(vmem_limit_bytes=12 << 20),
        cost_estimate=BRIEF,
    )(info, feats, feats, kv_in, edge0, edge1, taps)


def toeplitz_kernel(chunk, rate_row, coef_row, *rest):
    out = rest[-1]
    lag = (LANES - 1 - iota((LANES, LANES), 1)).astype(F32)
    rate = jnp.broadcast_to(rate_row[...], (LANES, LANES)).T
    coef = jnp.broadcast_to(coef_row[...], (LANES, LANES)).T
    taps = jnp.sum((coef * jnp.exp(-rate * lag)).reshape(PER_TILE, ORDER, LANES), axis=1)
    valid = iota((LANES, LANES), 1) <= iota((LANES, LANES), 0)
    for g in range(PER_TILE):
        spread = jnp.broadcast_to(taps[g : g + 1], (8, LANES))
        top = pltpu.roll(spread, 1, 1, stride=1, stride_axis=0)
        block = jnp.concatenate([top] + [pltpu.roll(top, at, 1) for at in range(8, chunk, 8)], axis=0)
        block = jnp.where(valid[:chunk], block, 0.0)
        out[g * chunk : (g + 1) * chunk, :] = block[:, :chunk].astype(BF16)


def toeplitz(rate_row, coef_row, chunk, first_tile, tiles, made=None):
    made = [] if made is None else [made]
    return pl.pallas_call(
        functools.partial(toeplitz_kernel, chunk),
        grid=(tiles,),
        in_specs=[pl.BlockSpec((1, LANES), lambda i: (0, first_tile + i))] * 2 + [pl.BlockSpec(memory_space=pl.ANY)] * len(made),
        out_specs=pl.BlockSpec((PER_TILE * chunk, chunk), lambda i: (first_tile + i, 0)),
        out_shape=jax.ShapeDtypeStruct((rate_row.shape[1] // GROUP_CH * chunk, chunk), BF16),
        input_output_aliases={2: 0} if made else {},
        cost_estimate=BRIEF,
    )(rate_row, coef_row, *made)


def local_kernel(prod, toep, out):
    rows, width = out.shape[0] // 2, out.shape[1]
    lane_group = iota((rows, LANES), 1) // GROUP_CH
    for w in range(width // LANES):
        lanes = slice(w * LANES, (w + 1) * LANES)
        beside = jnp.concatenate([prod[:rows, lanes], prod[rows : 2 * rows, lanes]], axis=1)
        local = dot(toep[w * PER_TILE * rows : (w + 1) * PER_TILE * rows, :], beside)
        for i in range(2):
            cols = slice(i * LANES, (i + 1) * LANES)
            kept = local[:rows, cols]
            for g in range(1, PER_TILE):
                kept = jnp.where(lane_group == g, local[g * rows : (g + 1) * rows, cols], kept)
            out[i * rows : (i + 1) * rows, lanes] = kept


def local(prod, toep):
    rows, width = toep.shape[1], prod.shape[1]
    block = min(512, width)
    return pl.pallas_call(
        local_kernel,
        grid=(width // block,),
        in_specs=[
            pl.BlockSpec((prod.shape[0], block), lambda i: (0, i)),
            pl.BlockSpec((block // GROUP_CH * rows, rows), lambda i: (i, 0)),
        ],
        out_specs=pl.BlockSpec((2 * rows, block), lambda i: (0, i)),
        out_shape=jax.ShapeDtypeStruct((2 * rows, width), F32),
        compiler_params=pltpu.CompilerParams(vmem_limit_bytes=12 << 20),
        cost_estimate=BRIEF,
    )(prod, toep)


def weight_copies(weights, part, cols, held, sems):
    share = held.shape[2]
    return [
        pltpu.make_async_copy(weights.at[:, pl.ds(part * cols + j * share, share)], held.at[j], sems.at[j])
        for j in range(held.shape[0])
    ]


def multiply(gated, copies, held, theirs, mine):
    rows, share = theirs.shape[0], held.shape[2]
    for j, copy in enumerate(copies):
        copy.wait()
        product = dot(gated, held[j])
        theirs[:, j * share : (j + 1) * share] = product[:rows].astype(BF16)
        mine[:, j * share : (j + 1) * share] = product[rows:].astype(BF16)


def gate_kernel(d, chips, info, local, inner, q0, q1, *rest):
    steps = 2 * chips
    ends, states, rest = rest[:steps], rest[steps : steps + chips], rest[steps + chips :]
    taps, before, wide_rates, rate_row, coef_row, weights, out, theirs, mine, pad, gated, held, sems = rest
    rows, width = q0.shape[-2:]
    cols = theirs.shape[1]
    step = min(64, rows)
    mask = own_group()
    later = (iota((rows, LANES), 0) + 1).astype(F32)
    places = [source(info[0], 2 * d + 1, chips), source(info[0], 2 * d, chips)]
    turn = pl.program_id(0)
    copies = weight_copies(weights, 0, cols, held, sems)

    @pl.when(turn == 0)
    def _():
        for copy in copies:
            copy.start()

    for w in range(width // LANES):
        lanes = slice(w * LANES, (w + 1) * LANES)
        into_high, into_low = halves(coef_row[:, lanes] * jnp.exp(-rate_row[:, lanes] * later))
        by_chip = []
        for y in range(chips):
            value = states[0][:, lanes]
            for i in range(1, chips):
                value = jnp.where((info[0] // 2 + chips - i) % chips == y, states[i][:, lanes], value)
            by_chip.append(value)
        rate = wide_rates[:, lanes]
        fade = jnp.exp(-rate * float(2 * rows))
        state = before[:, lanes]
        for y in range(chips - 1):
            state = jnp.where(y < places[0] // 2, fade * state + by_chip[y][:ORDER], state)
        halfway = inner[0:ORDER, lanes].astype(F32) + inner[ORDER:, lanes].astype(F32)
        halfway = jnp.exp(-rate * float(rows)) * state + halfway
        entering = [jnp.where(place % 2 == 0, state, halfway) for place in places]
        entering = [jnp.where(mask, jnp.concatenate([value] * PER_TILE, axis=0), 0.0) for value in entering]
        state_high, state_low = halves(jnp.concatenate(entering, axis=1))
        carried = dot(into_high, state_high) + dot(into_high, state_low) + dot(into_low, state_high)
        tap = taps[0, :, lanes]
        for i, (q, place) in enumerate(zip((q0, q1), places)):
            tail = by_chip[0][ORDER:]
            for e, end in enumerate(ends):
                rows_before = (end[0, :, lanes] if e == 0 else end[:, lanes]).astype(F32)[EDGE:]
                tail = jnp.where(source(info[0], e, chips) == place - 1, rows_before, tail)
            pad[w, i, 0:EDGE, :] = tail
            pad[w, i, EDGE:, :] = (q[0, :, lanes] if d == 0 and i == 1 else q[:, lanes]).astype(F32)
            base = pl.multiple_of((place % 2) * rows, rows)
            for start in range(0, rows, step):
                long = local[pl.ds(base + start, step), lanes] + carried[start : start + step, i * LANES : (i + 1) * LANES]
                value = convolve(pad.at[w, i], tap, start, step) * long
                at = i * rows + start
                gated[turn, at : at + step, lanes] = value.astype(BF16)

    @pl.when(turn == pl.num_programs(0) - 1)
    def _():
        whole = jnp.concatenate([gated[i] for i in range(gated.shape[0])], axis=1)
        out[...] = whole
        multiply(whole, copies, held, theirs, mine)


def gate(info, d, chips, local, prod, feats, pieces, states, taps, before, wide_rates, rate_row, coef_row, weights, parts):
    rows = feats.shape[1]
    width = taps.shape[2]
    steps = 2 * chips
    cols = weights.shape[1] // parts
    block = min(512, width)
    per = width // block
    share = min(512, cols)

    def spec(*shape):
        return pl.BlockSpec(shape + (block,), lambda i, info: (0,) * len(shape) + (i,))

    def of_own(count):
        at = rows // count - 1
        return pl.BlockSpec((1, count, block), lambda i, info: (0, at, info[0] * per + i))

    def of_piece(count):
        at = rows // count - 1
        return pl.BlockSpec((count, block), lambda i, info: (at, i))

    def whole(*shape):
        return pl.BlockSpec(shape, lambda i, info: (0,) * len(shape))

    pair = [pieces[2 * d], pieces[2 * d - 1]] if d > 0 else [pieces[0], feats]
    return pl.pallas_call(
        functools.partial(gate_kernel, d, chips),
        grid_spec=pltpu.PrefetchScalarGridSpec(
            num_scalar_prefetch=1,
            grid=(per,),
            in_specs=[spec(2 * rows), pl.BlockSpec((2 * ORDER, block), lambda i, info: (rows // ORDER, i))]
            + [of_piece(rows), of_piece(rows) if d > 0 else of_own(rows), of_own(2 * EDGE)]
            + [of_piece(2 * EDGE)] * (steps - 1)
            + [spec(ORDER + EDGE)] * chips
            + [spec(3, TAPS), spec(ORDER), spec(ORDER), spec(1), spec(1)]
            + [pl.BlockSpec(memory_space=pltpu.HBM)],
            out_specs=[whole(2 * rows, width), whole(rows, cols), whole(rows, cols)],
            scratch_shapes=[
                pltpu.VMEM((block // LANES, 2, EDGE + rows, LANES), F32),
                pltpu.VMEM((per, 2 * rows, block), BF16),
                pltpu.VMEM((cols // share, width, share), BF16),
                pltpu.SemaphoreType.DMA((cols // share,)),
            ],
        ),
        out_shape=[
            jax.ShapeDtypeStruct((2 * rows, width), BF16),
            jax.ShapeDtypeStruct((rows, cols), BF16),
            jax.ShapeDtypeStruct((rows, cols), BF16),
        ],
        compiler_params=pltpu.CompilerParams(vmem_limit_bytes=20 << 20),
        cost_estimate=BRIEF,
    )(info, local, prod, *pair, feats, *pieces, *states, taps, before, wide_rates, rate_row, coef_row, weights)


def project_kernel(part, gated, weights, theirs, mine, held, sems):
    copies = weight_copies(weights, part, theirs.shape[1], held, sems)
    for copy in copies:
        copy.start()
    multiply(gated[...], copies, held, theirs, mine)


def project(gated, weights, part, parts):
    rows, width = gated.shape[0] // 2, gated.shape[1]
    cols = weights.shape[1] // parts
    share = min(512, cols)
    vmem = pl.BlockSpec(memory_space=pltpu.VMEM)
    return pl.pallas_call(
        functools.partial(project_kernel, part),
        in_specs=[vmem, pl.BlockSpec(memory_space=pltpu.HBM)],
        out_specs=[vmem] * 2,
        out_shape=[jax.ShapeDtypeStruct((rows, cols), BF16)] * 2,
        scratch_shapes=[pltpu.VMEM((cols // share, width, share), BF16), pltpu.SemaphoreType.DMA((cols // share,))],
        compiler_params=pltpu.CompilerParams(vmem_limit_bytes=20 << 20),
        cost_estimate=BRIEF,
    )(gated, weights)


def finish_kernel(part, count, base, *rest):
    terms, (out, ready, sems) = rest[:count], rest[-3:]
    rows, cols = base.shape
    step = min(32, rows)
    copies = []
    for i in range(rows // step):
        span = slice(i * step, (i + 1) * step)
        total = base[span, :]
        for term in terms:
            total = total + term[span, :].astype(F32)
        ready[span, :] = total.astype(BF16)
        here = ready.at[pl.ds(i * step, step), :]
        copies.append(pltpu.make_async_copy(here, out.at[pl.ds(i * step, step), pl.ds(part * cols, cols)], sems.at[i]))
        copies[-1].start()
    for copy in copies:
        copy.wait()


def finish(part, parts, base, terms, out):
    rows, cols = base.shape
    before = [] if out is None else [out]
    vmem = pl.BlockSpec(memory_space=pltpu.VMEM)
    hbm = pl.BlockSpec(memory_space=pltpu.HBM)
    return pl.pallas_call(
        functools.partial(finish_kernel, part, len(terms)),
        in_specs=[vmem] * (1 + len(terms)) + [hbm] * len(before),
        out_specs=hbm,
        out_shape=jax.ShapeDtypeStruct((rows, cols * parts), BF16),
        scratch_shapes=[pltpu.VMEM((rows, cols), BF16), pltpu.SemaphoreType.DMA((rows // min(32, rows),))],
        input_output_aliases={1 + len(terms): 0} if before else {},
        compiler_params=pltpu.CompilerParams(vmem_limit_bytes=12 << 20),
        cost_estimate=BRIEF,
    )(base, *terms, *before)


def body(chips, contexts, features, residual, short_weight, rates, residues, out_weight):
    rows, _, depth = features.shape
    width = short_weight.shape[2]
    steps = 2 * chips
    chip_rows = 2 * rows
    context_rows = steps * rows
    tp, ctx = lax.axis_index("tp"), lax.axis_index("ctx")
    chip = tp // 2
    info = tp.astype(jnp.int32).reshape(1)
    always = tp < steps

    def send(value, e):
        return lax.ppermute(value, "tp", [(i, target(i, e, chips)) for i in range(steps)])

    def send_back(value, e):
        return lax.ppermute(value, "tp", [(i, source(i, e, chips)) for i in range(steps)])

    def with_context(value, bit):
        return lax.ppermute(value, "ctx", [(i, i ^ bit) for i in range(contexts)])

    def in_hbm(value):
        return pltpu.with_memory_space_constraint(value, pltpu.HBM)

    feats = in_hbm(jnp.transpose(features, (1, 0, 2)))
    taps = in_hbm(jnp.transpose(short_weight, (1, 0, 2)))
    poles = [in_hbm(jnp.transpose(value)) for value in (rates, residues)]
    kv_out, edge0, edge1, kv_taps, rate_row, coef_row, wide_rates, *pieces = first(info, feats, taps, *poles, chips)
    tiles = width // LANES
    early = tiles // 2
    toep = toeplitz(rate_row, coef_row, rows, 0, early)

    kv_taps = [kv_taps] + [send_back(kv_taps, 2 * d) for d in range(1, chips)]

    order = [(x * chips + y) * 2 for x in range(contexts) for y in range(chips)]
    edges = [
        lax.ppermute(part, ("ctx", "tp"), [(here + 1, after + c) for here, after in zip(order[:-1], order[1:])])
        for c, part in ((0, edge0), (1, edge1))
    ]

    kv_in = send(kv_out, 1)
    pieces[:chips] = [send(piece, e) for e, piece in enumerate(pieces[:chips], 1)]
    kv_in, edges, pieces[:chips], toep = lax.optimization_barrier((kv_in, edges, pieces[:chips], toep))

    prods, states = [None] * chips, [None] * chips
    for d in list(range(1, chips)) + [0]:
        prods[d], states[d] = front(info, d, chips, feats, kv_in, *edges, kv_taps[d])
        if d > 0:
            states[d] = send(states[d], 2 * d)
    states, prods, pieces[chips:] = lax.optimization_barrier((states, prods, pieces[chips:]))
    prods[1:] = [send(prods[d], 2 * d) for d in range(1, chips)]
    pieces[chips:] = [send(piece, e) for e, piece in enumerate(pieces[chips:], chips + 1)]

    def relay(states, prod, toep):
        by_chip = [
            sum(jnp.where((chip - d) % chips == y, state[:ORDER], 0.0) for d, state in enumerate(states))
            for y in range(chips)
        ]
        bits = [1 << i for i in range(contexts.bit_length() - 1)]
        fade = jnp.exp(-wide_rates * float(chip_rows))
        pasts = [jnp.exp(-wide_rates * float(bit * context_rows)) for bit in bits]
        places = [
            jnp.where((ctx & bit) != 0, jnp.exp(-wide_rates * ((ctx & (bit - 1)).astype(F32) * context_rows)), 0.0)
            for bit in bits
        ]
        total = by_chip[0]
        for y in range(1, chips):
            total = fade * total + by_chip[y]
        total, pasts, places = lax.optimization_barrier((total, pasts, places))
        before = jnp.zeros_like(total)
        for i, bit in enumerate(bits):
            got = with_context(total, bit)
            before = before + places[i] * got
            total = jnp.where((ctx & bit) != 0, pasts[i] * got + total, pasts[i] * total + got)
            if i == 0:
                toep = toeplitz(rate_row, coef_row, rows, early, tiles - early, toep)
                total, toep = lax.optimization_barrier((total, toep))
            if i == 1:
                near = local(prod, toep)
                total, near = lax.optimization_barrier((total, near))
        return before, near, toep

    def no_relay(states, prod, toep):
        return wide_rates, jnp.zeros((chip_rows, width), F32), toep

    before, near, toep = lax.cond(always, relay, no_relay, states, prods[0], toep)

    parts = 2
    cols = depth // parts
    weights = in_hbm(out_weight)

    def projected(d):
        inside = local(prods[d], toep) if d > 0 else near
        gated, theirs, mine = gate(
            info, d, chips, inside, prods[d], feats, pieces, states, taps, before, wide_rates, rate_row, coef_row,
            weights, parts,
        )
        sums = []
        for p in range(parts):
            if p > 0:
                theirs, mine = project(gated, weights, p, parts)
            sums.append(mine.astype(F32) + send(theirs, 1).astype(F32))
        return sums

    arriving = [[] for _ in range(parts)]
    for d in range(1, chips):
        for p, value in enumerate(projected(d)):
            arriving[p].append(send_back(value.astype(BF16), 2 * d))

    def own():
        return [
            value + residual[:, p * cols : (p + 1) * cols].astype(F32) for p, value in enumerate(projected(0))
        ]

    bases = lax.cond(always, own, lambda: [jnp.zeros((rows, cols), F32)] * parts)
    out = None
    for p in range(parts):
        out = finish(p, parts, bases[p], arriving[p], out)
    return out


def solution(mesh):
    chips, contexts = mesh.shape["tp"] // 2, mesh.shape["ctx"]
    in_specs = (
        P(("ctx", "tp"), None, None),
        P(("ctx", "tp"), None),
        P(None, None, "tp"),
        P("tp", None),
        P("tp", None),
        P("tp", None),
    )
    return jax.shard_map(
        functools.partial(body, chips, contexts),
        mesh=mesh,
        in_specs=in_specs,
        out_specs=P(("ctx", "tp"), None),
        check_vma=False,
    )
```

```python
import functools
import math

import jax
import jax.numpy as jnp
from jax import lax
from jax.experimental import pallas as pl
from jax.experimental.pallas import tpu as pltpu
from jax.sharding import PartitionSpec as P

ORDER = 16
GROUP_CH = 16
LANES = 128
TAPS = 7
EDGE = 8
F32 = jnp.float32
BF16 = jnp.bfloat16
PER_TILE = LANES // GROUP_CH
BRIEF = pl.CostEstimate(flops=1, bytes_accessed=1, transcendentals=0)


def halves(value):
    high = value.astype(BF16)
    return high, (value - high.astype(F32)).astype(BF16)


def dot(a, b):
    return jnp.dot(a, b, preferred_element_type=F32)


def iota(shape, dim):
    return lax.broadcasted_iota(jnp.int32, shape, dim)


def own_group():
    return iota((LANES, LANES), 0) // ORDER == iota((LANES, LANES), 1) // GROUP_CH


def target(position, e, chips):
    return 2 * ((position // 2 + e // 2) % chips) + (position % 2 + e % 2) % 2


def source(position, e, chips):
    return 2 * ((position // 2 + chips - e // 2) % chips) + (position % 2 + e % 2) % 2


def fold(product, mask):
    kept = jnp.where(mask, product, 0.0)
    return jnp.sum(kept.reshape(PER_TILE, ORDER, LANES), axis=0)


def convolve(padded, taps, start, count):
    total = taps[0:1] * padded[EDGE + start : EDGE + start + count]
    for j in range(1, TAPS):
        total = total + taps[j : j + 1] * padded[EDGE - j + start : EDGE - j + start + count]
    return total


def first_kernel(chips, info, feats, taps_in, rates_in, residues_in, kv_out, edge0, edge1, kv_taps, rate_row, coef_row, wide, *rest):
    steps = 2 * chips
    pieces, (last, taps, rates, residues, sems) = rest[: steps - 1], rest[steps - 1 :]
    rows, width = pieces[0].shape
    core = info[0] % 2
    copies = [(rates_in, rates), (residues_in, residues), (taps_in, taps), (feats.at[:, pl.ds(rows - 2 * EDGE, 2 * EDGE), :], last)]
    for j in range(chips):
        start = pl.multiple_of((2 * j + 1 - core) * width, LANES)
        for branch in range(2):
            copies.append((feats.at[branch + 1, :, pl.ds(start, width)], kv_out.at[branch, :, pl.ds(j * width, width)]))
    for e, piece in enumerate(pieces, 1):
        start = pl.multiple_of(target(info[0], e, chips) * width, LANES)
        copies.append((feats.at[0, :, pl.ds(start, width)], piece))
    copies = [pltpu.make_async_copy(*ends, sems.at[i]) for i, ends in enumerate(copies)]
    for copy in copies:
        copy.start()
    for copy in copies[:3]:
        copy.wait()

    rate, residue = rates[...], residues[...]
    coef = residue * jnp.sqrt(1.0 - jnp.exp(-2.0 * rate))
    lane_group = iota((ORDER, LANES), 1) // GROUP_CH
    diagonal = iota((ORDER, LANES), 1) % ORDER == iota((ORDER, LANES), 0)

    def spread(values, tile):
        out = jnp.broadcast_to(values[:, tile * PER_TILE : tile * PER_TILE + 1], (ORDER, LANES))
        for g in range(1, PER_TILE):
            at = tile * PER_TILE + g
            out = jnp.where(lane_group == g, jnp.broadcast_to(values[:, at : at + 1], (ORDER, LANES)), out)
        return out

    for b in range(2):
        kv_taps[b, 0:TAPS, :] = taps[b + 1]
    for tile in range(width // LANES):
        lanes = slice(tile * LANES, (tile + 1) * LANES)
        wide_rate = spread(rate, tile)
        wide[:, lanes] = wide_rate
        row = jnp.sum(jnp.where(diagonal, wide_rate, 0.0), axis=0, keepdims=True)
        rate_row[:, lanes] = row
        coef_row[:, lanes] = jnp.sum(jnp.where(diagonal, spread(coef, tile), 0.0), axis=0, keepdims=True)
        for b in range(2):
            kv_taps[b, TAPS : TAPS + 1, lanes] = row
    for copy in copies[3:]:
        copy.wait()
    for c, out in ((0, edge0), (1, edge1)):
        for j in range(chips):
            cols = slice((2 * j + c) * width, (2 * j + c + 1) * width)
            for branch in range(3):
                out[branch, :, j * width : (j + 1) * width] = last[branch, :, cols].astype(F32)[EDGE:].astype(BF16)


def first(info, feats, taps, rates, residues, chips):
    _, rows, depth = feats.shape
    width = taps.shape[2]
    others = 2 * chips - 1
    vmem = pl.BlockSpec(memory_space=pltpu.VMEM)
    return pl.pallas_call(
        functools.partial(first_kernel, chips),
        out_shape=[
            jax.ShapeDtypeStruct((2, rows, chips * width), BF16),
            jax.ShapeDtypeStruct((3, EDGE, chips * width), BF16),
            jax.ShapeDtypeStruct((3, EDGE, chips * width), BF16),
            jax.ShapeDtypeStruct((2, TAPS + 1, width), F32),
            jax.ShapeDtypeStruct((1, width), F32),
            jax.ShapeDtypeStruct((1, width), F32),
            jax.ShapeDtypeStruct((ORDER, width), F32),
        ]
        + [jax.ShapeDtypeStruct((rows, width), BF16)] * others,
        in_specs=[pl.BlockSpec(memory_space=pltpu.SMEM)] + [pl.BlockSpec(memory_space=pltpu.HBM)] * 4,
        out_specs=[vmem] * (7 + others),
        scratch_shapes=[
            pltpu.VMEM((3, 2 * EDGE, depth), BF16),
            pltpu.VMEM(taps.shape, F32),
            pltpu.VMEM(rates.shape, F32),
            pltpu.VMEM(residues.shape, F32),
            pltpu.SemaphoreType.DMA((4 + 2 * chips + others,)),
        ],
        compiler_params=pltpu.CompilerParams(vmem_limit_bytes=12 << 20),
        cost_estimate=BRIEF,
    )(info, feats, taps, rates, residues)


def front_kernel(info, k_own, v_own, kv_in, edge0, edge1, taps, prod, state, pad_k, pad_v):
    rows, width = k_own.shape[1:]
    core = info[0] % 2
    chip_rows = 2 * rows
    mine = pl.multiple_of(EDGE + core * rows, 8)
    other = pl.multiple_of(EDGE + (1 - core) * rows, 8)
    step = min(64, chip_rows)
    mask = own_group()
    age = (rows - 1 - iota((LANES, rows), 1)).astype(F32)
    for w in range(width // LANES):
        lanes = slice(w * LANES, (w + 1) * LANES)
        for b, own, pad in ((0, k_own, pad_k), (1, v_own, pad_v)):
            pad[w, 0:EDGE, :] = edge0[b + 1, :, lanes].astype(F32) + edge1[b + 1, :, lanes].astype(F32)
            pad[w, pl.ds(mine, rows), :] = own[0, :, lanes].astype(F32)
            pad[w, pl.ds(other, rows), :] = kv_in[b, :, lanes].astype(F32)
        tap_k, tap_v = taps[0, :, lanes], taps[1, :, lanes]
        for start in range(0, chip_rows, step):
            value = convolve(pad_k.at[w], tap_k, start, step) * convolve(pad_v.at[w], tap_v, start, step)
            prod[start : start + step, lanes] = value.astype(BF16)
        rate = jnp.broadcast_to(tap_k[TAPS : TAPS + 1], (LANES, LANES)).T
        high, low = halves(jnp.exp(-rate[:, :rows] * age))
        beside = jnp.concatenate([prod[0:rows, lanes], prod[rows:chip_rows, lanes]], axis=1)
        reached = dot(jnp.concatenate([high, low], axis=0), beside)
        reached = reached[:LANES] + reached[LANES:]
        inner_high, inner_low = halves(fold(reached[:, :LANES], mask))
        prod[chip_rows : chip_rows + ORDER, lanes] = inner_high
        prod[chip_rows + ORDER : chip_rows + 2 * ORDER, lanes] = inner_low
        state[0:ORDER, lanes] = fold(jnp.exp(-rate * float(rows)) * reached[:, :LANES] + reached[:, LANES:], mask)
        state[ORDER : ORDER + EDGE, lanes] = edge0[0, :, lanes].astype(F32) + edge1[0, :, lanes].astype(F32)


def front(info, d, chips, feats, kv_in, edge0, edge1, taps):
    rows = feats.shape[1]
    width = taps.shape[2]
    block = min(512, width)
    per = width // block
    stored = 2 * rows + 2 * ORDER

    def chip(info):
        return (info[0] // 2 + d) % chips

    def own(branch):
        return pl.BlockSpec((1, rows, block), lambda i, info: (branch, 0, (2 * chip(info) + info[0] % 2) * per + i))

    def of_chip(*shape):
        return pl.BlockSpec(shape + (block,), lambda i, info: (0,) * len(shape) + (chip(info) * per + i,))

    def spec(*shape):
        return pl.BlockSpec(shape + (block,), lambda i, info: (0,) * len(shape) + (i,))

    return pl.pallas_call(
        front_kernel,
        grid_spec=pltpu.PrefetchScalarGridSpec(
            num_scalar_prefetch=1,
            grid=(per,),
            in_specs=[own(1), own(2), of_chip(2, rows), of_chip(3, EDGE), of_chip(3, EDGE), spec(2, TAPS + 1)],
            out_specs=[spec(stored), spec(ORDER + EDGE)],
            scratch_shapes=[pltpu.VMEM((block // LANES, EDGE + 2 * rows, LANES), F32)] * 2,
        ),
        out_shape=[jax.ShapeDtypeStruct((stored, width), BF16), jax.ShapeDtypeStruct((ORDER + EDGE, width), F32)],
        compiler_params=pltpu.CompilerParams(vmem_limit_bytes=12 << 20),
        cost_estimate=BRIEF,
    )(info, feats, feats, kv_in, edge0, edge1, taps)


def toeplitz_kernel(chunk, rate_row, coef_row, *rest):
    out = rest[-1]
    lag = (LANES - 1 - iota((LANES, LANES), 1)).astype(F32)
    valid = iota((chunk, LANES), 1) <= iota((chunk, LANES), 0)
    for w in range(rate_row.shape[1] // LANES):
        lanes = slice(w * LANES, (w + 1) * LANES)
        rate = jnp.broadcast_to(rate_row[:, lanes], (LANES, LANES)).T
        coef = jnp.broadcast_to(coef_row[:, lanes], (LANES, LANES)).T
        taps = jnp.sum((coef * jnp.exp(-rate * lag)).reshape(PER_TILE, ORDER, LANES), axis=1)
        for g in range(PER_TILE):
            spread = jnp.broadcast_to(taps[g : g + 1], (8, LANES))
            top = pltpu.roll(spread, 1, 1, stride=1, stride_axis=0)
            block = jnp.concatenate([top] + [pltpu.roll(top, at, 1) for at in range(8, chunk, 8)], axis=0)
            at = (w * PER_TILE + g) * chunk
            out[at : at + chunk, :] = jnp.where(valid, block, 0.0)[:, :chunk].astype(BF16)


def toeplitz(rate_row, coef_row, chunk, first_tile, tiles, made=None):
    made = [] if made is None else [made]
    together = 4 if tiles % 4 == 0 and first_tile % 4 == 0 else 1
    at = first_tile // together
    return pl.pallas_call(
        functools.partial(toeplitz_kernel, chunk),
        grid=(tiles // together,),
        in_specs=[pl.BlockSpec((1, together * LANES), lambda i: (0, at + i))] * 2 + [pl.BlockSpec(memory_space=pl.ANY)] * len(made),
        out_specs=pl.BlockSpec((together * PER_TILE * chunk, chunk), lambda i: (at + i, 0)),
        out_shape=jax.ShapeDtypeStruct((rate_row.shape[1] // GROUP_CH * chunk, chunk), BF16),
        input_output_aliases={2: 0} if made else {},
        cost_estimate=BRIEF,
    )(rate_row, coef_row, *made)


def weight_copies(weights, first, held, sems):
    share = held.shape[2]
    return [
        pltpu.make_async_copy(weights.at[:, pl.ds(first + j * share, share)], held.at[j], sems.at[j])
        for j in range(held.shape[0])
    ]


def multiply(gated, copies, held, theirs, mine):
    rows, share = theirs.shape[0], held.shape[2]
    for j, copy in enumerate(copies):
        copy.wait()
        product = dot(gated, held[j])
        theirs[:, j * share : (j + 1) * share] = product[:rows].astype(BF16)
        mine[:, j * share : (j + 1) * share] = product[rows:].astype(BF16)


def gate_kernel(d, chips, info, prod, toep, q0, q1, *rest):
    states, rest = rest[:chips], rest[chips:]
    taps, before, wide_rates, rate_row, coef_row, weights, out, theirs, mine, pad, gated, held, sems = rest
    rows, width = q0.shape[-2:]
    step = min(64, rows)
    mask = own_group()
    later = (iota((rows, LANES), 0) + 1).astype(F32)
    places = [source(info[0], 2 * d + 1, chips), source(info[0], 2 * d, chips)]
    begins = [pl.multiple_of((place % 2) * rows, rows) for place in places]
    lane_group = iota((step, LANES), 1) // GROUP_CH
    turn = pl.program_id(0)
    copies = weight_copies(weights, 0, held, sems)

    @pl.when(turn == 0)
    def _():
        for copy in copies:
            copy.start()

    for w in range(width // LANES):
        lanes = slice(w * LANES, (w + 1) * LANES)
        into_high, into_low = halves(coef_row[:, lanes] * jnp.exp(-rate_row[:, lanes] * later))
        by_chip = []
        for y in range(chips):
            value = states[0][:, lanes]
            for i in range(1, chips):
                value = jnp.where((info[0] // 2 + chips - i) % chips == y, states[i][:, lanes], value)
            by_chip.append(value)
        rate = wide_rates[:, lanes]
        fade = jnp.exp(-rate * float(2 * rows))
        state = before[:, lanes]
        for y in range(chips - 1):
            state = jnp.where(y < places[0] // 2, fade * state + by_chip[y][:ORDER], state)
        inner = prod[2 * rows :, lanes].astype(F32)
        halfway = inner[:ORDER] + inner[ORDER:]
        halfway = jnp.exp(-rate * float(rows)) * state + halfway
        entering = [jnp.where(place % 2 == 0, state, halfway) for place in places]
        entering = [jnp.where(mask, jnp.concatenate([value] * PER_TILE, axis=0), 0.0) for value in entering]
        state_high, state_low = halves(jnp.concatenate(entering, axis=1))
        carried = dot(into_high, state_high) + dot(into_high, state_low) + dot(into_low, state_high)
        beside = jnp.concatenate([prod[pl.ds(at, rows), lanes] for at in begins], axis=1)
        local = dot(toep[w * PER_TILE * rows : (w + 1) * PER_TILE * rows, :], beside)
        tap = taps[0, :, lanes]
        for i, (q, place) in enumerate(zip((q0, q1), places)):
            other = (q1, q0)[i]
            other = (other[0, rows - 2 * EDGE :, lanes] if d == 0 and i == 0 else other[rows - 2 * EDGE :, lanes]).astype(F32)
            pad[w, i, 0:EDGE, :] = jnp.where(place % 2 == 0, states[d][ORDER:, lanes], other[EDGE:])
            pad[w, i, EDGE:, :] = (q[0, :, lanes] if d == 0 and i == 1 else q[:, lanes]).astype(F32)
            cols_of = slice(i * LANES, (i + 1) * LANES)
            for start in range(0, rows, step):
                long = local[start : start + step, cols_of]
                for g in range(1, PER_TILE):
                    long = jnp.where(lane_group == g, local[g * rows + start : g * rows + start + step, cols_of], long)
                long = long + carried[start : start + step, cols_of]
                value = convolve(pad.at[w, i], tap, start, step) * long
                at = i * rows + start
                gated[turn, at : at + step, lanes] = value.astype(BF16)

    @pl.when(turn == pl.num_programs(0) - 1)
    def _():
        whole = jnp.concatenate([gated[i] for i in range(gated.shape[0])], axis=1)
        out[...] = whole
        multiply(whole, copies, held, theirs, mine)


def gate(info, d, chips, prod, toep, feats, pieces, states, taps, before, wide_rates, rate_row, coef_row, weights, cols):
    rows = feats.shape[1]
    width = taps.shape[2]
    block = min(512, width)
    per = width // block
    share = min(512, cols)

    def spec(*shape):
        return pl.BlockSpec(shape + (block,), lambda i, info: (0,) * len(shape) + (i,))

    def whole(*shape):
        return pl.BlockSpec(shape, lambda i, info: (0,) * len(shape))

    pair = [pieces[2 * d], pieces[2 * d - 1]] if d > 0 else [pieces[0], feats]
    return pl.pallas_call(
        functools.partial(gate_kernel, d, chips),
        grid_spec=pltpu.PrefetchScalarGridSpec(
            num_scalar_prefetch=1,
            grid=(per,),
            in_specs=[spec(2 * rows + 2 * ORDER), pl.BlockSpec((block // GROUP_CH * rows, rows), lambda i, info: (i, 0))]
            + [spec(rows), spec(rows) if d > 0 else pl.BlockSpec((1, rows, block), lambda i, info: (0, 0, info[0] * per + i))]
            + [spec(ORDER + EDGE)] * chips
            + [spec(3, TAPS), spec(ORDER), spec(ORDER), spec(1), spec(1)]
            + [pl.BlockSpec(memory_space=pltpu.HBM)],
            out_specs=[whole(2 * rows, width), whole(rows, cols), whole(rows, cols)],
            scratch_shapes=[
                pltpu.VMEM((block // LANES, 2, EDGE + rows, LANES), F32),
                pltpu.VMEM((per, 2 * rows, block), BF16),
                pltpu.VMEM((cols // share, width, share), BF16),
                pltpu.SemaphoreType.DMA((cols // share,)),
            ],
        ),
        out_shape=[
            jax.ShapeDtypeStruct((2 * rows, width), BF16),
            jax.ShapeDtypeStruct((rows, cols), BF16),
            jax.ShapeDtypeStruct((rows, cols), BF16),
        ],
        compiler_params=pltpu.CompilerParams(vmem_limit_bytes=24 << 20),
        cost_estimate=BRIEF,
    )(info, prod, toep, *pair, *states, taps, before, wide_rates, rate_row, coef_row, weights)


def project_kernel(first, gated, weights, theirs, mine, held, sems):
    copies = weight_copies(weights, first, held, sems)
    for copy in copies:
        copy.start()
    multiply(gated[...], copies, held, theirs, mine)


def project(gated, weights, first, cols):
    rows, width = gated.shape[0] // 2, gated.shape[1]
    share = min(512, cols)
    vmem = pl.BlockSpec(memory_space=pltpu.VMEM)
    return pl.pallas_call(
        functools.partial(project_kernel, first),
        in_specs=[vmem, pl.BlockSpec(memory_space=pltpu.HBM)],
        out_specs=[vmem] * 2,
        out_shape=[jax.ShapeDtypeStruct((rows, cols), BF16)] * 2,
        scratch_shapes=[pltpu.VMEM((cols // share, width, share), BF16), pltpu.SemaphoreType.DMA((cols // share,))],
        compiler_params=pltpu.CompilerParams(vmem_limit_bytes=20 << 20),
        cost_estimate=BRIEF,
    )(gated, weights)


def finish_kernel(first, blocks, count, *rest):
    bases, terms, (out, ready, sems) = rest[:blocks], rest[blocks : blocks + count], rest[-3:]
    rows, cols = ready.shape
    step = min(32, rows)
    copies = []
    for i in range(rows // step):
        span = slice(i * step, (i + 1) * step)
        total = jnp.concatenate([base[span, :] for base in bases], axis=1)
        for term in terms:
            total = total + term[span, :].astype(F32)
        ready[span, :] = total.astype(BF16)
        here = ready.at[pl.ds(i * step, step), :]
        copies.append(pltpu.make_async_copy(here, out.at[pl.ds(i * step, step), pl.ds(first, cols)], sems.at[i]))
        copies[-1].start()
    for copy in copies:
        copy.wait()


def finish(first, cols, base, terms, out):
    rows, depth = base.shape
    before = [] if out is None else [out]
    block = math.gcd(first, cols)
    vmem = pl.BlockSpec(memory_space=pltpu.VMEM)
    hbm = pl.BlockSpec(memory_space=pltpu.HBM)
    return pl.pallas_call(
        functools.partial(finish_kernel, first, cols // block, len(terms)),
        grid=(1,),
        in_specs=[pl.BlockSpec((rows, block), lambda i, at=first // block + j: (0, at)) for j in range(cols // block)]
        + [vmem] * len(terms)
        + [hbm] * len(before),
        out_specs=hbm,
        out_shape=jax.ShapeDtypeStruct((rows, depth), BF16),
        scratch_shapes=[pltpu.VMEM((rows, cols), BF16), pltpu.SemaphoreType.DMA((rows // min(32, rows),))],
        input_output_aliases={cols // block + len(terms): 0} if before else {},
        compiler_params=pltpu.CompilerParams(vmem_limit_bytes=12 << 20),
        cost_estimate=BRIEF,
    )(*[base] * (cols // block), *terms, *before)


def body(chips, contexts, features, residual, short_weight, rates, residues, out_weight):
    rows, _, depth = features.shape
    width = short_weight.shape[2]
    steps = 2 * chips
    chip_rows = 2 * rows
    context_rows = steps * rows
    tp, ctx = lax.axis_index("tp"), lax.axis_index("ctx")
    chip = tp // 2
    info = tp.astype(jnp.int32).reshape(1)
    always = tp < steps

    def send(value, e):
        return lax.ppermute(value, "tp", [(i, target(i, e, chips)) for i in range(steps)])

    def send_back(value, e):
        return lax.ppermute(value, "tp", [(i, source(i, e, chips)) for i in range(steps)])

    def with_context(value, bit):
        return lax.ppermute(value, "ctx", [(i, i ^ bit) for i in range(contexts)])

    def in_hbm(value):
        return pltpu.with_memory_space_constraint(value, pltpu.HBM)

    feats = in_hbm(jnp.transpose(features, (1, 0, 2)))
    taps = in_hbm(jnp.transpose(short_weight, (1, 0, 2)))
    poles = [in_hbm(jnp.transpose(value)) for value in (rates, residues)]
    kv_out, edge0, edge1, kv_taps, rate_row, coef_row, wide_rates, *pieces = first(info, feats, taps, *poles, chips)
    tiles = width // LANES
    early = tiles // 2

    kv_taps = [kv_taps] + [send_back(kv_taps, 2 * d) for d in range(1, chips)]

    order = [(x * chips + y) * 2 for x in range(contexts) for y in range(chips)]
    edges = [
        lax.ppermute(part, ("ctx", "tp"), [(here + 1, after + c) for here, after in zip(order[:-1], order[1:])])
        for c, part in ((0, edge0), (1, edge1))
    ]

    kv_in = send(kv_out, 1)
    kv_in, edges, kv_taps, pieces = lax.optimization_barrier((kv_in, edges, kv_taps, pieces))
    pieces[:chips] = [send(piece, e) for e, piece in enumerate(pieces[:chips], 1)]

    prods, states = [None] * chips, [None] * chips
    for d in list(range(1, chips)) + [0]:
        prods[d], states[d] = front(info, d, chips, feats, kv_in, *edges, kv_taps[d])
        if d > 0:
            states[d] = send(states[d], 2 * d)
    states, prods, pieces = lax.optimization_barrier((states, prods, pieces))
    prods[1:] = [send(prods[d], 2 * d) for d in range(1, chips)]
    pieces[chips:] = [send(piece, e) for e, piece in enumerate(pieces[chips:], chips + 1)]

    def relay(states):
        by_chip = [
            sum(jnp.where((chip - d) % chips == y, state[:ORDER], 0.0) for d, state in enumerate(states))
            for y in range(chips)
        ]
        bits = [1 << i for i in range(contexts.bit_length() - 1)]
        fade = jnp.exp(-wide_rates * float(chip_rows))
        pasts = [jnp.exp(-wide_rates * float(bit * context_rows)) for bit in bits]
        places = [
            jnp.where((ctx & bit) != 0, jnp.exp(-wide_rates * ((ctx & (bit - 1)).astype(F32) * context_rows)), 0.0)
            for bit in bits
        ]
        total = by_chip[0]
        for y in range(1, chips):
            total = fade * total + by_chip[y]
        total, pasts, places = lax.optimization_barrier((total, pasts, places))
        before = jnp.zeros_like(total)
        for i, bit in enumerate(bits):
            got = with_context(total, bit)
            before = before + places[i] * got
            total = jnp.where((ctx & bit) != 0, pasts[i] * got + total, pasts[i] * total + got)
            if i == 0:
                toep = toeplitz(rate_row, coef_row, rows, 0, early)
                total, toep = lax.optimization_barrier((total, toep))
            if i == 1:
                toep = toeplitz(rate_row, coef_row, rows, early, tiles - early, toep)
                total, toep = lax.optimization_barrier((total, toep))
        return before, toep

    def no_relay(states):
        return wide_rates, jnp.zeros((width // GROUP_CH * rows, rows), BF16)

    before, toep = lax.cond(always, relay, no_relay, states)

    parts = [(0, depth // 4), (depth // 4, 3 * depth // 8), (5 * depth // 8, 3 * depth // 8)]
    weights = in_hbm(out_weight)

    def gated_rows(d, prod, cols):
        return gate(
            info, d, chips, prod, toep, feats, pieces, states, taps, before, wide_rates, rate_row, coef_row,
            weights, cols,
        )

    def summed(theirs, mine):
        return mine.astype(F32) + send(theirs, 1).astype(F32)

    def own(prod):
        _, theirs, mine = gated_rows(0, prod, depth)
        return residual.astype(F32) + summed(theirs, mine)

    def no_own(prod):
        return jnp.zeros((rows, depth), F32)

    gateds, wholes, arriving = [], [], []
    for d in range(1, chips):
        gated, *first_part = gated_rows(d, prods[d], parts[0][1])
        gateds.append(gated)
        wholes.append(summed(*first_part).astype(BF16))
    for part in parts[1:]:

        def others(gateds, part=part):
            return [summed(*project(gated, weights, *part)).astype(BF16) for gated in gateds]

        def no_others(gateds, part=part):
            return [jnp.zeros((rows, part[1]), BF16) for _ in gateds]

        gateds, wholes = lax.optimization_barrier((gateds, wholes))
        arriving.append([send_back(whole, 2 * d) for d, whole in enumerate(wholes, 1)])
        wholes = lax.cond(always, others, no_others, gateds)
    prods[0], wholes, arriving[0] = lax.optimization_barrier((prods[0], wholes, arriving[0]))
    arriving.append([send_back(whole, 2 * d) for d, whole in enumerate(wholes, 1)])
    base = lax.cond(always, own, no_own, prods[0])
    out = None
    for (first_col, cols), terms in zip(parts, arriving):
        out = finish(first_col, cols, base, terms, out)
    return out


def solution(mesh):
    chips, contexts = mesh.shape["tp"] // 2, mesh.shape["ctx"]
    in_specs = (
        P(("ctx", "tp"), None, None),
        P(("ctx", "tp"), None),
        P(None, None, "tp"),
        P("tp", None),
        P("tp", None),
        P("tp", None),
    )
    return jax.shard_map(
        functools.partial(body, chips, contexts),
        mesh=mesh,
        in_specs=in_specs,
        out_specs=P(("ctx", "tp"), None),
        check_vma=False,
    )
```

```python
import functools

import jax
import jax.numpy as jnp
from jax import lax
from jax.experimental import pallas as pl
from jax.experimental.pallas import tpu as pltpu
from jax.sharding import PartitionSpec as P

ORDER = 16
GROUP_CH = 16
LANES = 128
TAPS = 7
EDGE = 8
F32 = jnp.float32
BF16 = jnp.bfloat16
PER_TILE = LANES // GROUP_CH
BRIEF = pl.CostEstimate(flops=1, bytes_accessed=1, transcendentals=0)


def halves(value):
    high = value.astype(BF16)
    return high, (value - high.astype(F32)).astype(BF16)


def dot(a, b):
    return jnp.dot(a, b, preferred_element_type=F32)


def iota(shape, dim):
    return lax.broadcasted_iota(jnp.int32, shape, dim)


def own_group():
    return iota((LANES, LANES), 0) // ORDER == iota((LANES, LANES), 1) // GROUP_CH


def target(position, e, chips):
    return 2 * ((position // 2 + e // 2) % chips) + (position % 2 + e % 2) % 2


def source(position, e, chips):
    return 2 * ((position // 2 + chips - e // 2) % chips) + (position % 2 + e % 2) % 2


def fold(product, mask):
    kept = jnp.where(mask, product, 0.0)
    return jnp.sum(kept.reshape(PER_TILE, ORDER, LANES), axis=0)


def convolve(padded, taps, start, count):
    total = taps[0:1] * padded[EDGE + start : EDGE + start + count]
    for j in range(1, TAPS):
        total = total + taps[j : j + 1] * padded[EDGE - j + start : EDGE - j + start + count]
    return total


def first_kernel(chips, info, feats, taps_in, rates_in, residues_in, kv_out, edge0, edge1, kv_taps, rate_row, coef_row, wide, *rest):
    steps = 2 * chips
    pieces, (last, taps, rates, residues, sems) = rest[: steps - 1], rest[steps - 1 :]
    rows, width = pieces[0].shape
    core = info[0] % 2
    copies = [(rates_in, rates), (residues_in, residues), (taps_in, taps), (feats.at[:, pl.ds(rows - 2 * EDGE, 2 * EDGE), :], last)]
    for j in range(chips):
        start = pl.multiple_of((2 * j + 1 - core) * width, LANES)
        for branch in range(2):
            copies.append((feats.at[branch + 1, :, pl.ds(start, width)], kv_out.at[branch, :, pl.ds(j * width, width)]))
    for e, piece in enumerate(pieces, 1):
        start = pl.multiple_of(target(info[0], e, chips) * width, LANES)
        copies.append((feats.at[0, :, pl.ds(start, width)], piece))
    copies = [pltpu.make_async_copy(*ends, sems.at[i]) for i, ends in enumerate(copies)]
    for copy in copies:
        copy.start()
    for copy in copies[:3]:
        copy.wait()

    rate, residue = rates[...], residues[...]
    coef = residue * jnp.sqrt(1.0 - jnp.exp(-2.0 * rate))
    lane_group = iota((ORDER, LANES), 1) // GROUP_CH
    diagonal = iota((ORDER, LANES), 1) % ORDER == iota((ORDER, LANES), 0)

    def spread(values, tile):
        out = jnp.broadcast_to(values[:, tile * PER_TILE : tile * PER_TILE + 1], (ORDER, LANES))
        for g in range(1, PER_TILE):
            at = tile * PER_TILE + g
            out = jnp.where(lane_group == g, jnp.broadcast_to(values[:, at : at + 1], (ORDER, LANES)), out)
        return out

    for b in range(2):
        kv_taps[b, 0:TAPS, :] = taps[b + 1]
    for tile in range(width // LANES):
        lanes = slice(tile * LANES, (tile + 1) * LANES)
        wide_rate = spread(rate, tile)
        wide[:, lanes] = wide_rate
        row = jnp.sum(jnp.where(diagonal, wide_rate, 0.0), axis=0, keepdims=True)
        rate_row[:, lanes] = row
        coef_row[:, lanes] = jnp.sum(jnp.where(diagonal, spread(coef, tile), 0.0), axis=0, keepdims=True)
        for b in range(2):
            kv_taps[b, TAPS : TAPS + 1, lanes] = row
    for copy in copies[3:]:
        copy.wait()
    for c, out in ((0, edge0), (1, edge1)):
        for j in range(chips):
            cols = slice((2 * j + c) * width, (2 * j + c + 1) * width)
            for branch in range(3):
                out[branch, :, j * width : (j + 1) * width] = last[branch, :, cols].astype(F32)[EDGE:].astype(BF16)


def first(info, feats, taps, rates, residues, chips):
    _, rows, depth = feats.shape
    width = taps.shape[2]
    others = 2 * chips - 1
    vmem = pl.BlockSpec(memory_space=pltpu.VMEM)
    return pl.pallas_call(
        functools.partial(first_kernel, chips),
        out_shape=[
            jax.ShapeDtypeStruct((2, rows, chips * width), BF16),
            jax.ShapeDtypeStruct((3, EDGE, chips * width), BF16),
            jax.ShapeDtypeStruct((3, EDGE, chips * width), BF16),
            jax.ShapeDtypeStruct((2, TAPS + 1, width), F32),
            jax.ShapeDtypeStruct((1, width), F32),
            jax.ShapeDtypeStruct((1, width), F32),
            jax.ShapeDtypeStruct((ORDER, width), F32),
        ]
        + [jax.ShapeDtypeStruct((rows, width), BF16)] * others,
        in_specs=[pl.BlockSpec(memory_space=pltpu.SMEM)] + [pl.BlockSpec(memory_space=pltpu.HBM)] * 4,
        out_specs=[vmem] * (7 + others),
        scratch_shapes=[
            pltpu.VMEM((3, 2 * EDGE, depth), BF16),
            pltpu.VMEM(taps.shape, F32),
            pltpu.VMEM(rates.shape, F32),
            pltpu.VMEM(residues.shape, F32),
            pltpu.SemaphoreType.DMA((4 + 2 * chips + others,)),
        ],
        compiler_params=pltpu.CompilerParams(vmem_limit_bytes=12 << 20),
        cost_estimate=BRIEF,
    )(info, feats, taps, rates, residues)


def front_kernel(info, k_own, v_own, kv_in, edge0, edge1, taps, prod, state, pad_k, pad_v):
    rows, width = k_own.shape[1:]
    core = info[0] % 2
    chip_rows = 2 * rows
    mine = pl.multiple_of(EDGE + core * rows, 8)
    other = pl.multiple_of(EDGE + (1 - core) * rows, 8)
    step = min(64, chip_rows)
    mask = own_group()
    age = (rows - 1 - iota((LANES, rows), 1)).astype(F32)
    for w in range(width // LANES):
        lanes = slice(w * LANES, (w + 1) * LANES)
        for b, own, pad in ((0, k_own, pad_k), (1, v_own, pad_v)):
            pad[w, 0:EDGE, :] = edge0[b + 1, :, lanes].astype(F32) + edge1[b + 1, :, lanes].astype(F32)
            pad[w, pl.ds(mine, rows), :] = own[0, :, lanes].astype(F32)
            pad[w, pl.ds(other, rows), :] = kv_in[b, :, lanes].astype(F32)
        tap_k, tap_v = taps[0, :, lanes], taps[1, :, lanes]
        for start in range(0, chip_rows, step):
            value = convolve(pad_k.at[w], tap_k, start, step) * convolve(pad_v.at[w], tap_v, start, step)
            prod[start : start + step, lanes] = value.astype(BF16)
        rate = jnp.broadcast_to(tap_k[TAPS : TAPS + 1], (LANES, LANES)).T
        high, low = halves(jnp.exp(-rate[:, :rows] * age))
        beside = jnp.concatenate([prod[0:rows, lanes], prod[rows:chip_rows, lanes]], axis=1)
        reached = dot(jnp.concatenate([high, low], axis=0), beside)
        reached = reached[:LANES] + reached[LANES:]
        inner_high, inner_low = halves(fold(reached[:, :LANES], mask))
        prod[chip_rows : chip_rows + ORDER, lanes] = inner_high
        prod[chip_rows + ORDER : chip_rows + 2 * ORDER, lanes] = inner_low
        state[0:ORDER, lanes] = fold(jnp.exp(-rate * float(rows)) * reached[:, :LANES] + reached[:, LANES:], mask)
        state[ORDER : ORDER + EDGE, lanes] = edge0[0, :, lanes].astype(F32) + edge1[0, :, lanes].astype(F32)


def front(info, d, chips, feats, kv_in, edge0, edge1, taps):
    rows = feats.shape[1]
    width = taps.shape[2]
    block = min(512, width)
    per = width // block
    stored = 2 * rows + 2 * ORDER

    def chip(info):
        return (info[0] // 2 + d) % chips

    def own(branch):
        return pl.BlockSpec((1, rows, block), lambda i, info: (branch, 0, (2 * chip(info) + info[0] % 2) * per + i))

    def of_chip(*shape):
        return pl.BlockSpec(shape + (block,), lambda i, info: (0,) * len(shape) + (chip(info) * per + i,))

    def spec(*shape):
        return pl.BlockSpec(shape + (block,), lambda i, info: (0,) * len(shape) + (i,))

    return pl.pallas_call(
        front_kernel,
        grid_spec=pltpu.PrefetchScalarGridSpec(
            num_scalar_prefetch=1,
            grid=(per,),
            in_specs=[own(1), own(2), of_chip(2, rows), of_chip(3, EDGE), of_chip(3, EDGE), spec(2, TAPS + 1)],
            out_specs=[spec(stored), spec(ORDER + EDGE)],
            scratch_shapes=[pltpu.VMEM((block // LANES, EDGE + 2 * rows, LANES), F32)] * 2,
        ),
        out_shape=[jax.ShapeDtypeStruct((stored, width), BF16), jax.ShapeDtypeStruct((ORDER + EDGE, width), F32)],
        compiler_params=pltpu.CompilerParams(vmem_limit_bytes=12 << 20),
        cost_estimate=BRIEF,
    )(info, feats, feats, kv_in, edge0, edge1, taps)


def toeplitz_kernel(chunk, rate_row, coef_row, *rest):
    out = rest[-1]
    lag = (LANES - 1 - iota((LANES, LANES), 1)).astype(F32)
    valid = iota((chunk, LANES), 1) <= iota((chunk, LANES), 0)
    for w in range(rate_row.shape[1] // LANES):
        lanes = slice(w * LANES, (w + 1) * LANES)
        rate = jnp.broadcast_to(rate_row[:, lanes], (LANES, LANES)).T
        coef = jnp.broadcast_to(coef_row[:, lanes], (LANES, LANES)).T
        taps = jnp.sum((coef * jnp.exp(-rate * lag)).reshape(PER_TILE, ORDER, LANES), axis=1)
        for g in range(PER_TILE):
            spread = jnp.broadcast_to(taps[g : g + 1], (8, LANES))
            top = pltpu.roll(spread, 1, 1, stride=1, stride_axis=0)
            block = jnp.concatenate([top] + [pltpu.roll(top, at, 1) for at in range(8, chunk, 8)], axis=0)
            at = (w * PER_TILE + g) * chunk
            out[at : at + chunk, :] = jnp.where(valid, block, 0.0)[:, :chunk].astype(BF16)


def toeplitz(rate_row, coef_row, chunk, first_tile, tiles, made=None):
    made = [] if made is None else [made]
    together = 4 if tiles % 4 == 0 and first_tile % 4 == 0 else 1
    at = first_tile // together
    return pl.pallas_call(
        functools.partial(toeplitz_kernel, chunk),
        grid=(tiles // together,),
        in_specs=[pl.BlockSpec((1, together * LANES), lambda i: (0, at + i))] * 2 + [pl.BlockSpec(memory_space=pl.ANY)] * len(made),
        out_specs=pl.BlockSpec((together * PER_TILE * chunk, chunk), lambda i: (at + i, 0)),
        out_shape=jax.ShapeDtypeStruct((rate_row.shape[1] // GROUP_CH * chunk, chunk), BF16),
        input_output_aliases={2: 0} if made else {},
        cost_estimate=BRIEF,
    )(rate_row, coef_row, *made)


def local_kernel(prod, toep, out):
    rows, width = out.shape[0] // 2, out.shape[1]
    lane_group = iota((rows, LANES), 1) // GROUP_CH
    for w in range(width // LANES):
        lanes = slice(w * LANES, (w + 1) * LANES)
        beside = jnp.concatenate([prod[:rows, lanes], prod[rows : 2 * rows, lanes]], axis=1)
        local = dot(toep[w * PER_TILE * rows : (w + 1) * PER_TILE * rows, :], beside)
        for i in range(2):
            cols = slice(i * LANES, (i + 1) * LANES)
            kept = local[:rows, cols]
            for g in range(1, PER_TILE):
                kept = jnp.where(lane_group == g, local[g * rows : (g + 1) * rows, cols], kept)
            out[i * rows : (i + 1) * rows, lanes] = kept


def local(prod, toep):
    rows, width = toep.shape[1], prod.shape[1]
    block = min(512, width)
    return pl.pallas_call(
        local_kernel,
        grid=(width // block,),
        in_specs=[
            pl.BlockSpec((prod.shape[0], block), lambda i: (0, i)),
            pl.BlockSpec((block // GROUP_CH * rows, rows), lambda i: (i, 0)),
        ],
        out_specs=pl.BlockSpec((2 * rows, block), lambda i: (0, i)),
        out_shape=jax.ShapeDtypeStruct((2 * rows, width), F32),
        compiler_params=pltpu.CompilerParams(vmem_limit_bytes=12 << 20),
        cost_estimate=BRIEF,
    )(prod, toep)


def weight_copies(weights, first, held, sems):
    share = held.shape[2]
    return [
        pltpu.make_async_copy(weights.at[:, pl.ds(first + j * share, share)], held.at[j], sems.at[j])
        for j in range(held.shape[0])
    ]


def multiply(gated, copies, held, theirs, mine):
    rows, share = theirs.shape[0], held.shape[2]
    for j, copy in enumerate(copies):
        copy.wait()
        product = dot(gated, held[j])
        theirs[:, j * share : (j + 1) * share] = product[:rows].astype(BF16)
        mine[:, j * share : (j + 1) * share] = product[rows:].astype(BF16)


def gate_kernel(d, chips, info, long_in, second, q0, q1, *rest):
    states, rest = rest[:chips], rest[chips:]
    taps, before, wide_rates, rate_row, coef_row, weights, out, theirs, mine, pad, gated, held, sems = rest
    rows, width = q0.shape[-2:]
    step = min(64, rows)
    mask = own_group()
    later = (iota((rows, LANES), 0) + 1).astype(F32)
    places = [source(info[0], 2 * d + 1, chips), source(info[0], 2 * d, chips)]
    begins = [pl.multiple_of((place % 2) * rows, rows) for place in places]
    lane_group = iota((step, LANES), 1) // GROUP_CH
    turn = pl.program_id(0)
    copies = weight_copies(weights, 0, held, sems)

    @pl.when(turn == 0)
    def _():
        for copy in copies:
            copy.start()

    for w in range(width // LANES):
        lanes = slice(w * LANES, (w + 1) * LANES)
        into_high, into_low = halves(coef_row[:, lanes] * jnp.exp(-rate_row[:, lanes] * later))
        by_chip = []
        for y in range(chips):
            value = states[0][:, lanes]
            for i in range(1, chips):
                value = jnp.where((info[0] // 2 + chips - i) % chips == y, states[i][:, lanes], value)
            by_chip.append(value)
        rate = wide_rates[:, lanes]
        fade = jnp.exp(-rate * float(2 * rows))
        state = before[:, lanes]
        for y in range(chips - 1):
            state = jnp.where(y < places[0] // 2, fade * state + by_chip[y][:ORDER], state)
        inner = (long_in[2 * rows :, lanes] if d == 0 else second[:, lanes]).astype(F32)
        halfway = inner[:ORDER] + inner[ORDER:]
        halfway = jnp.exp(-rate * float(rows)) * state + halfway
        entering = [jnp.where(place % 2 == 0, state, halfway) for place in places]
        entering = [jnp.where(mask, jnp.concatenate([value] * PER_TILE, axis=0), 0.0) for value in entering]
        state_high, state_low = halves(jnp.concatenate(entering, axis=1))
        carried = dot(into_high, state_high) + dot(into_high, state_low) + dot(into_low, state_high)
        if d == 0:
            beside = jnp.concatenate([long_in[pl.ds(at, rows), lanes] for at in begins], axis=1)
            local = dot(second[w * PER_TILE * rows : (w + 1) * PER_TILE * rows, :], beside)
        tap = taps[0, :, lanes]
        for i, (q, place) in enumerate(zip((q0, q1), places)):
            other = (q1, q0)[i]
            other = (other[0, rows - 2 * EDGE :, lanes] if d == 0 and i == 0 else other[rows - 2 * EDGE :, lanes]).astype(F32)
            pad[w, i, 0:EDGE, :] = jnp.where(place % 2 == 0, states[d][ORDER:, lanes], other[EDGE:])
            pad[w, i, EDGE:, :] = (q[0, :, lanes] if d == 0 and i == 1 else q[:, lanes]).astype(F32)
            cols_of = slice(i * LANES, (i + 1) * LANES)
            for start in range(0, rows, step):
                if d > 0:
                    long = long_in[pl.ds(begins[i] + start, step), lanes]
                else:
                    long = local[start : start + step, cols_of]
                    for g in range(1, PER_TILE):
                        at = g * rows + start
                        long = jnp.where(lane_group == g, local[at : at + step, cols_of], long)
                long = long + carried[start : start + step, cols_of]
                value = convolve(pad.at[w, i], tap, start, step) * long
                at = i * rows + start
                gated[turn, at : at + step, lanes] = value.astype(BF16)

    @pl.when(turn == pl.num_programs(0) - 1)
    def _():
        whole = jnp.concatenate([gated[i] for i in range(gated.shape[0])], axis=1)
        out[...] = whole
        multiply(whole, copies, held, theirs, mine)


def gate(info, d, chips, prod, toep, feats, pieces, states, taps, before, wide_rates, rate_row, coef_row, weights, cols):
    rows = feats.shape[1]
    width = taps.shape[2]
    block = min(512, width)
    per = width // block
    share = min(512, cols)

    def spec(*shape):
        return pl.BlockSpec(shape + (block,), lambda i, info: (0,) * len(shape) + (i,))

    def whole(*shape):
        return pl.BlockSpec(shape, lambda i, info: (0,) * len(shape))

    pair = [pieces[2 * d], pieces[2 * d - 1]] if d > 0 else [pieces[0], feats]
    return pl.pallas_call(
        functools.partial(gate_kernel, d, chips),
        grid_spec=pltpu.PrefetchScalarGridSpec(
            num_scalar_prefetch=1,
            grid=(per,),
            in_specs=(
                [spec(2 * rows), pl.BlockSpec((2 * ORDER, block), lambda i, info: (rows // ORDER, i))]
                if d > 0
                else [spec(2 * rows + 2 * ORDER), pl.BlockSpec((block // GROUP_CH * rows, rows), lambda i, info: (i, 0))]
            )
            + [spec(rows), spec(rows) if d > 0 else pl.BlockSpec((1, rows, block), lambda i, info: (0, 0, info[0] * per + i))]
            + [spec(ORDER + EDGE)] * chips
            + [spec(3, TAPS), spec(ORDER), spec(ORDER), spec(1), spec(1)]
            + [pl.BlockSpec(memory_space=pltpu.HBM)],
            out_specs=[whole(2 * rows, width), whole(rows, cols), whole(rows, cols)],
            scratch_shapes=[
                pltpu.VMEM((block // LANES, 2, EDGE + rows, LANES), F32),
                pltpu.VMEM((per, 2 * rows, block), BF16),
                pltpu.VMEM((cols // share, width, share), BF16),
                pltpu.SemaphoreType.DMA((cols // share,)),
            ],
        ),
        out_shape=[
            jax.ShapeDtypeStruct((2 * rows, width), BF16),
            jax.ShapeDtypeStruct((rows, cols), BF16),
            jax.ShapeDtypeStruct((rows, cols), BF16),
        ],
        compiler_params=pltpu.CompilerParams(vmem_limit_bytes=24 << 20),
        cost_estimate=BRIEF,
    )(info, *((local(prod, toep), prod) if d > 0 else (prod, toep)), *pair, *states, taps, before, wide_rates, rate_row, coef_row, weights)


def project_kernel(first, gated, weights, theirs, mine, held, sems):
    copies = weight_copies(weights, first, held, sems)
    for copy in copies:
        copy.start()
    multiply(gated[...], copies, held, theirs, mine)


def project(gated, weights, first, cols):
    rows, width = gated.shape[0] // 2, gated.shape[1]
    share = min(512, cols)
    vmem = pl.BlockSpec(memory_space=pltpu.VMEM)
    return pl.pallas_call(
        functools.partial(project_kernel, first),
        in_specs=[vmem, pl.BlockSpec(memory_space=pltpu.HBM)],
        out_specs=[vmem] * 2,
        out_shape=[jax.ShapeDtypeStruct((rows, cols), BF16)] * 2,
        scratch_shapes=[pltpu.VMEM((cols // share, width, share), BF16), pltpu.SemaphoreType.DMA((cols // share,))],
        compiler_params=pltpu.CompilerParams(vmem_limit_bytes=20 << 20),
        cost_estimate=BRIEF,
    )(gated, weights)


def finish_kernel(parts, base, *rest):
    terms, (out, ready, sems) = rest[:-3], rest[-3:]
    rows = base.shape[0]
    step = min(32, rows)
    each = len(terms) // len(parts)
    copies = []
    for i in range(rows // step):
        span = slice(i * step, (i + 1) * step)
        for p, (first, cols) in enumerate(parts):
            total = base[span, first : first + cols]
            for term in terms[p * each : (p + 1) * each]:
                total = total + term[span, :].astype(F32)
            ready[span, first : first + cols] = total.astype(BF16)
        here = pl.ds(i * step, step)
        copies.append(pltpu.make_async_copy(ready.at[here, :], out.at[here, :], sems.at[i]))
        copies[-1].start()
    for copy in copies:
        copy.wait()


def finish(parts, base, terms):
    rows, depth = base.shape
    return pl.pallas_call(
        functools.partial(finish_kernel, parts),
        in_specs=[pl.BlockSpec(memory_space=pltpu.VMEM)] * (1 + len(terms)),
        out_specs=pl.BlockSpec(memory_space=pltpu.HBM),
        out_shape=jax.ShapeDtypeStruct((rows, depth), BF16),
        scratch_shapes=[pltpu.VMEM((rows, depth), BF16), pltpu.SemaphoreType.DMA((rows // min(32, rows),))],
        compiler_params=pltpu.CompilerParams(vmem_limit_bytes=12 << 20),
        cost_estimate=BRIEF,
    )(base, *terms)


def body(chips, contexts, features, residual, short_weight, rates, residues, out_weight):
    rows, _, depth = features.shape
    width = short_weight.shape[2]
    steps = 2 * chips
    chip_rows = 2 * rows
    context_rows = steps * rows
    tp, ctx = lax.axis_index("tp"), lax.axis_index("ctx")
    chip = tp // 2
    info = tp.astype(jnp.int32).reshape(1)
    always = tp < steps

    def send(value, e):
        return lax.ppermute(value, "tp", [(i, target(i, e, chips)) for i in range(steps)])

    def send_back(value, e):
        return lax.ppermute(value, "tp", [(i, source(i, e, chips)) for i in range(steps)])

    def with_context(value, bit):
        return lax.ppermute(value, "ctx", [(i, i ^ bit) for i in range(contexts)])

    def in_hbm(value):
        return pltpu.with_memory_space_constraint(value, pltpu.HBM)

    feats = in_hbm(jnp.transpose(features, (1, 0, 2)))
    taps = in_hbm(jnp.transpose(short_weight, (1, 0, 2)))
    poles = [in_hbm(jnp.transpose(value)) for value in (rates, residues)]
    kv_out, edge0, edge1, kv_taps, rate_row, coef_row, wide_rates, *pieces = first(info, feats, taps, *poles, chips)
    tiles = width // LANES
    early = tiles // 2

    kv_taps = [kv_taps] + [send_back(kv_taps, 2 * d) for d in range(1, chips)]

    order = [(x * chips + y) * 2 for x in range(contexts) for y in range(chips)]
    edges = [
        lax.ppermute(part, ("ctx", "tp"), [(here + 1, after + c) for here, after in zip(order[:-1], order[1:])])
        for c, part in ((0, edge0), (1, edge1))
    ]

    kv_in = send(kv_out, 1)
    kv_in, edges, kv_taps, pieces = lax.optimization_barrier((kv_in, edges, kv_taps, pieces))
    pieces[:chips] = [send(piece, e) for e, piece in enumerate(pieces[:chips], 1)]

    prods, states = [None] * chips, [None] * chips
    for d in list(range(1, chips)) + [0]:
        prods[d], states[d] = front(info, d, chips, feats, kv_in, *edges, kv_taps[d])
        if d > 0:
            states[d] = send(states[d], 2 * d)
    states, prods, pieces = lax.optimization_barrier((states, prods, pieces))
    prods[1:] = [send(prods[d], 2 * d) for d in range(1, chips)]
    pieces[chips:] = [send(piece, e) for e, piece in enumerate(pieces[chips:], chips + 1)]

    def relay(states):
        by_chip = [
            sum(jnp.where((chip - d) % chips == y, state[:ORDER], 0.0) for d, state in enumerate(states))
            for y in range(chips)
        ]
        bits = [1 << i for i in range(contexts.bit_length() - 1)]
        fade = jnp.exp(-wide_rates * float(chip_rows))
        pasts = [jnp.exp(-wide_rates * float(bit * context_rows)) for bit in bits]
        places = [
            jnp.where((ctx & bit) != 0, jnp.exp(-wide_rates * ((ctx & (bit - 1)).astype(F32) * context_rows)), 0.0)
            for bit in bits
        ]
        total = by_chip[0]
        for y in range(1, chips):
            total = fade * total + by_chip[y]
        total, pasts, places = lax.optimization_barrier((total, pasts, places))
        before = jnp.zeros_like(total)
        for i, bit in enumerate(bits):
            got = with_context(total, bit)
            before = before + places[i] * got
            total = jnp.where((ctx & bit) != 0, pasts[i] * got + total, pasts[i] * total + got)
            if i == 0:
                toep = toeplitz(rate_row, coef_row, rows, 0, early)
                total, toep = lax.optimization_barrier((total, toep))
            if i == 1:
                toep = toeplitz(rate_row, coef_row, rows, early, tiles - early, toep)
                total, toep = lax.optimization_barrier((total, toep))
        return before, toep

    def no_relay(states):
        return wide_rates, jnp.zeros((width // GROUP_CH * rows, rows), BF16)

    before, toep = lax.cond(always, relay, no_relay, states)

    parts = [(0, depth // 4), (depth // 4, 3 * depth // 8), (5 * depth // 8, 3 * depth // 8)]
    weights = in_hbm(out_weight)

    def gated_rows(d, prod, cols):
        return gate(
            info, d, chips, prod, toep, feats, pieces, states, taps, before, wide_rates, rate_row, coef_row,
            weights, cols,
        )

    def summed(theirs, mine):
        return mine.astype(F32) + send(theirs, 1).astype(F32)

    def own(prod):
        half = depth // 2
        gated, *first_half = gated_rows(0, prod, half)
        sums = [summed(*first_half), summed(*project(gated, weights, half, half))]
        return residual.astype(F32) + jnp.concatenate(sums, axis=1)

    def no_own(prod):
        return jnp.zeros((rows, depth), F32)

    gateds, wholes, arriving = [], [], []
    for d in range(1, chips):
        gated, *first_part = gated_rows(d, prods[d], parts[0][1])
        gateds.append(gated)
        wholes.append(summed(*first_part).astype(BF16))
    for part in parts[1:]:

        def others(gateds, part=part):
            return [summed(*project(gated, weights, *part)).astype(BF16) for gated in gateds]

        def no_others(gateds, part=part):
            return [jnp.zeros((rows, part[1]), BF16) for _ in gateds]

        gateds, wholes = lax.optimization_barrier((gateds, wholes))
        arriving.append([send_back(whole, 2 * d) for d, whole in enumerate(wholes, 1)])
        wholes = lax.cond(always, others, no_others, gateds)
    prods[0], wholes, arriving[0] = lax.optimization_barrier((prods[0], wholes, arriving[0]))
    arriving.append([send_back(whole, 2 * d) for d, whole in enumerate(wholes, 1)])
    base = lax.cond(always, own, no_own, prods[0])
    return finish(parts, base, [term for terms in arriving for term in terms])


def solution(mesh):
    chips, contexts = mesh.shape["tp"] // 2, mesh.shape["ctx"]
    in_specs = (
        P(("ctx", "tp"), None, None),
        P(("ctx", "tp"), None),
        P(None, None, "tp"),
        P("tp", None),
        P("tp", None),
        P("tp", None),
    )
    return jax.shard_map(
        functools.partial(body, chips, contexts),
        mesh=mesh,
        in_specs=in_specs,
        out_specs=P(("ctx", "tp"), None),
        check_vma=False,
    )
```

```python
import functools

import jax
import jax.numpy as jnp
from jax import lax
from jax.experimental import pallas as pl
from jax.experimental.pallas import tpu as pltpu
from jax.sharding import PartitionSpec as P

ORDER = 16
GROUP_CH = 16
LANES = 128
TAPS = 7
EDGE = 8
F32 = jnp.float32
BF16 = jnp.bfloat16
PER_TILE = LANES // GROUP_CH
BRIEF = pl.CostEstimate(flops=1, bytes_accessed=1, transcendentals=0)


def halves(value):
    high = value.astype(BF16)
    return high, (value - high.astype(F32)).astype(BF16)


def dot(a, b):
    return jnp.dot(a, b, preferred_element_type=F32)


def iota(shape, dim):
    return lax.broadcasted_iota(jnp.int32, shape, dim)


def own_group():
    return iota((LANES, LANES), 0) // ORDER == iota((LANES, LANES), 1) // GROUP_CH


def target(position, e, chips):
    return 2 * ((position // 2 + e // 2) % chips) + (position % 2 + e % 2) % 2


def source(position, e, chips):
    return 2 * ((position // 2 + chips - e // 2) % chips) + (position % 2 + e % 2) % 2


def fold(product, mask):
    kept = jnp.where(mask, product, 0.0)
    return jnp.sum(kept.reshape(PER_TILE, ORDER, LANES), axis=0)


def convolve(padded, taps, start, count):
    total = taps[0:1] * padded[EDGE + start : EDGE + start + count]
    for j in range(1, TAPS):
        total = total + taps[j : j + 1] * padded[EDGE - j + start : EDGE - j + start + count]
    return total


def first_kernel(chips, info, feats, taps_in, rates_in, residues_in, kv_out, edge0, edge1, kv_taps, rate_row, coef_row, wide, *rest):
    steps = 2 * chips
    pieces, (last, taps, rates, residues, sems) = rest[: steps - 1], rest[steps - 1 :]
    rows, width = pieces[0].shape
    core = info[0] % 2
    copies = [(rates_in, rates), (residues_in, residues), (taps_in, taps), (feats.at[:, pl.ds(rows - 2 * EDGE, 2 * EDGE), :], last)]
    for j in range(chips):
        start = pl.multiple_of((2 * j + 1 - core) * width, LANES)
        for branch in range(2):
            copies.append((feats.at[branch + 1, :, pl.ds(start, width)], kv_out.at[branch, :, pl.ds(j * width, width)]))
    for e, piece in enumerate(pieces, 1):
        start = pl.multiple_of(target(info[0], e, chips) * width, LANES)
        copies.append((feats.at[0, :, pl.ds(start, width)], piece))
    copies = [pltpu.make_async_copy(*ends, sems.at[i]) for i, ends in enumerate(copies)]
    for copy in copies:
        copy.start()
    for copy in copies[:3]:
        copy.wait()

    rate, residue = rates[...], residues[...]
    coef = residue * jnp.sqrt(1.0 - jnp.exp(-2.0 * rate))
    lane_group = iota((ORDER, LANES), 1) // GROUP_CH
    diagonal = iota((ORDER, LANES), 1) % ORDER == iota((ORDER, LANES), 0)

    def spread(values, tile):
        out = jnp.broadcast_to(values[:, tile * PER_TILE : tile * PER_TILE + 1], (ORDER, LANES))
        for g in range(1, PER_TILE):
            at = tile * PER_TILE + g
            out = jnp.where(lane_group == g, jnp.broadcast_to(values[:, at : at + 1], (ORDER, LANES)), out)
        return out

    for b in range(2):
        kv_taps[b, 0:TAPS, :] = taps[b + 1]
    for tile in range(width // LANES):
        lanes = slice(tile * LANES, (tile + 1) * LANES)
        wide_rate = spread(rate, tile)
        wide[:, lanes] = wide_rate
        row = jnp.sum(jnp.where(diagonal, wide_rate, 0.0), axis=0, keepdims=True)
        rate_row[:, lanes] = row
        coef_row[:, lanes] = jnp.sum(jnp.where(diagonal, spread(coef, tile), 0.0), axis=0, keepdims=True)
        for b in range(2):
            kv_taps[b, TAPS : TAPS + 1, lanes] = row
    for copy in copies[3:]:
        copy.wait()
    for c, out in ((0, edge0), (1, edge1)):
        for j in range(chips):
            cols = slice((2 * j + c) * width, (2 * j + c + 1) * width)
            for branch in range(3):
                out[branch, :, j * width : (j + 1) * width] = last[branch, :, cols].astype(F32)[EDGE:].astype(BF16)


def first(info, feats, taps, rates, residues, chips):
    _, rows, depth = feats.shape
    width = taps.shape[2]
    others = 2 * chips - 1
    vmem = pl.BlockSpec(memory_space=pltpu.VMEM)
    return pl.pallas_call(
        functools.partial(first_kernel, chips),
        out_shape=[
            jax.ShapeDtypeStruct((2, rows, chips * width), BF16),
            jax.ShapeDtypeStruct((3, EDGE, chips * width), BF16),
            jax.ShapeDtypeStruct((3, EDGE, chips * width), BF16),
            jax.ShapeDtypeStruct((2, TAPS + 1, width), F32),
            jax.ShapeDtypeStruct((1, width), F32),
            jax.ShapeDtypeStruct((1, width), F32),
            jax.ShapeDtypeStruct((ORDER, width), F32),
        ]
        + [jax.ShapeDtypeStruct((rows, width), BF16)] * others,
        in_specs=[pl.BlockSpec(memory_space=pltpu.SMEM)] + [pl.BlockSpec(memory_space=pltpu.HBM)] * 4,
        out_specs=[vmem] * (7 + others),
        scratch_shapes=[
            pltpu.VMEM((3, 2 * EDGE, depth), BF16),
            pltpu.VMEM(taps.shape, F32),
            pltpu.VMEM(rates.shape, F32),
            pltpu.VMEM(residues.shape, F32),
            pltpu.SemaphoreType.DMA((4 + 2 * chips + others,)),
        ],
        compiler_params=pltpu.CompilerParams(vmem_limit_bytes=12 << 20),
        cost_estimate=BRIEF,
    )(info, feats, taps, rates, residues)


def front_kernel(info, k_own, v_own, kv_in, edge0, edge1, taps, prod, state, pad_k, pad_v):
    rows, width = k_own.shape[1:]
    core = info[0] % 2
    chip_rows = 2 * rows
    mine = pl.multiple_of(EDGE + core * rows, 8)
    other = pl.multiple_of(EDGE + (1 - core) * rows, 8)
    step = min(64, chip_rows)
    mask = own_group()
    age = (rows - 1 - iota((LANES, rows), 1)).astype(F32)
    for w in range(width // LANES):
        lanes = slice(w * LANES, (w + 1) * LANES)
        for b, own, pad in ((0, k_own, pad_k), (1, v_own, pad_v)):
            pad[w, 0:EDGE, :] = edge0[b + 1, :, lanes].astype(F32) + edge1[b + 1, :, lanes].astype(F32)
            pad[w, pl.ds(mine, rows), :] = own[0, :, lanes].astype(F32)
            pad[w, pl.ds(other, rows), :] = kv_in[b, :, lanes].astype(F32)
        tap_k, tap_v = taps[0, :, lanes], taps[1, :, lanes]
        for start in range(0, chip_rows, step):
            value = convolve(pad_k.at[w], tap_k, start, step) * convolve(pad_v.at[w], tap_v, start, step)
            prod[start : start + step, lanes] = value.astype(BF16)
        rate = jnp.broadcast_to(tap_k[TAPS : TAPS + 1], (LANES, LANES)).T
        high, low = halves(jnp.exp(-rate[:, :rows] * age))
        beside = jnp.concatenate([prod[0:rows, lanes], prod[rows:chip_rows, lanes]], axis=1)
        reached = dot(jnp.concatenate([high, low], axis=0), beside)
        reached = reached[:LANES] + reached[LANES:]
        inner_high, inner_low = halves(fold(reached[:, :LANES], mask))
        prod[chip_rows : chip_rows + ORDER, lanes] = inner_high
        prod[chip_rows + ORDER : chip_rows + 2 * ORDER, lanes] = inner_low
        state[0:ORDER, lanes] = fold(jnp.exp(-rate * float(rows)) * reached[:, :LANES] + reached[:, LANES:], mask)
        state[ORDER : ORDER + EDGE, lanes] = edge0[0, :, lanes].astype(F32) + edge1[0, :, lanes].astype(F32)


def front(info, d, chips, feats, kv_in, edge0, edge1, taps):
    rows = feats.shape[1]
    width = taps.shape[2]
    block = min(512, width)
    per = width // block
    stored = 2 * rows + 2 * ORDER

    def chip(info):
        return (info[0] // 2 + d) % chips

    def own(branch):
        return pl.BlockSpec((1, rows, block), lambda i, info: (branch, 0, (2 * chip(info) + info[0] % 2) * per + i))

    def of_chip(*shape):
        return pl.BlockSpec(shape + (block,), lambda i, info: (0,) * len(shape) + (chip(info) * per + i,))

    def spec(*shape):
        return pl.BlockSpec(shape + (block,), lambda i, info: (0,) * len(shape) + (i,))

    return pl.pallas_call(
        front_kernel,
        grid_spec=pltpu.PrefetchScalarGridSpec(
            num_scalar_prefetch=1,
            grid=(per,),
            in_specs=[own(1), own(2), of_chip(2, rows), of_chip(3, EDGE), of_chip(3, EDGE), spec(2, TAPS + 1)],
            out_specs=[spec(stored), spec(ORDER + EDGE)],
            scratch_shapes=[pltpu.VMEM((block // LANES, EDGE + 2 * rows, LANES), F32)] * 2,
        ),
        out_shape=[jax.ShapeDtypeStruct((stored, width), BF16), jax.ShapeDtypeStruct((ORDER + EDGE, width), F32)],
        compiler_params=pltpu.CompilerParams(vmem_limit_bytes=12 << 20),
        cost_estimate=BRIEF,
    )(info, feats, feats, kv_in, edge0, edge1, taps)


def toeplitz_kernel(chunk, rate_row, coef_row, *rest):
    out = rest[-1]
    lag = (LANES - 1 - iota((LANES, LANES), 1)).astype(F32)
    valid = iota((chunk, LANES), 1) <= iota((chunk, LANES), 0)
    for w in range(rate_row.shape[1] // LANES):
        lanes = slice(w * LANES, (w + 1) * LANES)
        rate = jnp.broadcast_to(rate_row[:, lanes], (LANES, LANES)).T
        coef = jnp.broadcast_to(coef_row[:, lanes], (LANES, LANES)).T
        taps = jnp.sum((coef * jnp.exp(-rate * lag)).reshape(PER_TILE, ORDER, LANES), axis=1)
        for g in range(PER_TILE):
            spread = jnp.broadcast_to(taps[g : g + 1], (8, LANES))
            top = pltpu.roll(spread, 1, 1, stride=1, stride_axis=0)
            block = jnp.concatenate([top] + [pltpu.roll(top, at, 1) for at in range(8, chunk, 8)], axis=0)
            at = (w * PER_TILE + g) * chunk
            out[at : at + chunk, :] = jnp.where(valid, block, 0.0)[:, :chunk].astype(BF16)


def toeplitz(rate_row, coef_row, chunk, first_tile, tiles, made=None):
    made = [] if made is None else [made]
    together = 4 if tiles % 4 == 0 and first_tile % 4 == 0 else 1
    at = first_tile // together
    return pl.pallas_call(
        functools.partial(toeplitz_kernel, chunk),
        grid=(tiles // together,),
        in_specs=[pl.BlockSpec((1, together * LANES), lambda i: (0, at + i))] * 2 + [pl.BlockSpec(memory_space=pl.ANY)] * len(made),
        out_specs=pl.BlockSpec((together * PER_TILE * chunk, chunk), lambda i: (at + i, 0)),
        out_shape=jax.ShapeDtypeStruct((rate_row.shape[1] // GROUP_CH * chunk, chunk), BF16),
        input_output_aliases={2: 0} if made else {},
        cost_estimate=BRIEF,
    )(rate_row, coef_row, *made)


def local_kernel(prod, toep, out):
    rows, width = out.shape[0] // 2, out.shape[1]
    lane_group = iota((rows, LANES), 1) // GROUP_CH
    for w in range(width // LANES):
        lanes = slice(w * LANES, (w + 1) * LANES)
        beside = jnp.concatenate([prod[:rows, lanes], prod[rows : 2 * rows, lanes]], axis=1)
        local = dot(toep[w * PER_TILE * rows : (w + 1) * PER_TILE * rows, :], beside)
        for i in range(2):
            cols = slice(i * LANES, (i + 1) * LANES)
            kept = local[:rows, cols]
            for g in range(1, PER_TILE):
                kept = jnp.where(lane_group == g, local[g * rows : (g + 1) * rows, cols], kept)
            out[i * rows : (i + 1) * rows, lanes] = kept


def local(prod, toep):
    rows, width = toep.shape[1], prod.shape[1]
    block = min(512, width)
    return pl.pallas_call(
        local_kernel,
        grid=(width // block,),
        in_specs=[
            pl.BlockSpec((prod.shape[0], block), lambda i: (0, i)),
            pl.BlockSpec((block // GROUP_CH * rows, rows), lambda i: (i, 0)),
        ],
        out_specs=pl.BlockSpec((2 * rows, block), lambda i: (0, i)),
        out_shape=jax.ShapeDtypeStruct((2 * rows, width), F32),
        compiler_params=pltpu.CompilerParams(vmem_limit_bytes=12 << 20),
        cost_estimate=BRIEF,
    )(prod, toep)


def weight_copies(weights, first, held, sems):
    share = held.shape[2]
    return [
        pltpu.make_async_copy(weights.at[:, pl.ds(first + j * share, share)], held.at[j], sems.at[j])
        for j in range(held.shape[0])
    ]


def multiply(gated, copies, held, theirs, mine):
    rows, share = theirs.shape[0], held.shape[2]
    for j, copy in enumerate(copies):
        copy.wait()
        product = dot(gated, held[j])
        theirs[:, j * share : (j + 1) * share] = product[:rows].astype(BF16)
        mine[:, j * share : (j + 1) * share] = product[rows:].astype(BF16)


def gate_kernel(d, chips, info, long_in, second, q0, q1, *rest):
    states, rest = rest[:chips], rest[chips:]
    taps, before, wide_rates, rate_row, coef_row, weights, out, theirs, mine, pad, gated, held, sems = rest
    rows, width = q0.shape[-2:]
    step = min(64, rows)
    mask = own_group()
    later = (iota((rows, LANES), 0) + 1).astype(F32)
    places = [source(info[0], 2 * d + 1, chips), source(info[0], 2 * d, chips)]
    begins = [pl.multiple_of((place % 2) * rows, rows) for place in places]
    lane_group = iota((step, LANES), 1) // GROUP_CH
    turn = pl.program_id(0)
    copies = weight_copies(weights, 0, held, sems)

    @pl.when(turn == 0)
    def _():
        for copy in copies:
            copy.start()

    for w in range(width // LANES):
        lanes = slice(w * LANES, (w + 1) * LANES)
        into_high, into_low = halves(coef_row[:, lanes] * jnp.exp(-rate_row[:, lanes] * later))
        by_chip = []
        for y in range(chips):
            value = states[0][:, lanes]
            for i in range(1, chips):
                value = jnp.where((info[0] // 2 + chips - i) % chips == y, states[i][:, lanes], value)
            by_chip.append(value)
        rate = wide_rates[:, lanes]
        fade = jnp.exp(-rate * float(2 * rows))
        state = before[:, lanes]
        for y in range(chips - 1):
            state = jnp.where(y < places[0] // 2, fade * state + by_chip[y][:ORDER], state)
        inner = (long_in[2 * rows :, lanes] if d == 0 else second[:, lanes]).astype(F32)
        halfway = inner[:ORDER] + inner[ORDER:]
        halfway = jnp.exp(-rate * float(rows)) * state + halfway
        entering = [jnp.where(place % 2 == 0, state, halfway) for place in places]
        entering = [jnp.where(mask, jnp.concatenate([value] * PER_TILE, axis=0), 0.0) for value in entering]
        state_high, state_low = halves(jnp.concatenate(entering, axis=1))
        carried = dot(into_high, state_high) + dot(into_high, state_low) + dot(into_low, state_high)
        if d == 0:
            beside = jnp.concatenate([long_in[pl.ds(at, rows), lanes] for at in begins], axis=1)
            local = dot(second[w * PER_TILE * rows : (w + 1) * PER_TILE * rows, :], beside)
        tap = taps[0, :, lanes]
        for i, (q, place) in enumerate(zip((q0, q1), places)):
            other = (q1, q0)[i]
            other = (other[0, rows - 2 * EDGE :, lanes] if d == 0 and i == 0 else other[rows - 2 * EDGE :, lanes]).astype(F32)
            pad[w, i, 0:EDGE, :] = jnp.where(place % 2 == 0, states[d][ORDER:, lanes], other[EDGE:])
            pad[w, i, EDGE:, :] = (q[0, :, lanes] if d == 0 and i == 1 else q[:, lanes]).astype(F32)
            cols_of = slice(i * LANES, (i + 1) * LANES)
            for start in range(0, rows, step):
                if d > 0:
                    long = long_in[pl.ds(begins[i] + start, step), lanes]
                else:
                    long = local[start : start + step, cols_of]
                    for g in range(1, PER_TILE):
                        at = g * rows + start
                        long = jnp.where(lane_group == g, local[at : at + step, cols_of], long)
                long = long + carried[start : start + step, cols_of]
                value = convolve(pad.at[w, i], tap, start, step) * long
                at = i * rows + start
                gated[turn, at : at + step, lanes] = value.astype(BF16)

    @pl.when(turn == pl.num_programs(0) - 1)
    def _():
        whole = jnp.concatenate([gated[i] for i in range(gated.shape[0])], axis=1)
        out[...] = whole
        multiply(whole, copies, held, theirs, mine)


def gate(info, d, chips, prod, toep, feats, pieces, states, taps, before, wide_rates, rate_row, coef_row, weights, cols):
    rows = feats.shape[1]
    width = taps.shape[2]
    block = min(512, width)
    per = width // block
    share = min(512, cols)

    def spec(*shape):
        return pl.BlockSpec(shape + (block,), lambda i, info: (0,) * len(shape) + (i,))

    def whole(*shape):
        return pl.BlockSpec(shape, lambda i, info: (0,) * len(shape))

    pair = [pieces[2 * d], pieces[2 * d - 1]] if d > 0 else [pieces[0], feats]
    return pl.pallas_call(
        functools.partial(gate_kernel, d, chips),
        grid_spec=pltpu.PrefetchScalarGridSpec(
            num_scalar_prefetch=1,
            grid=(per,),
            in_specs=(
                [spec(2 * rows), pl.BlockSpec((2 * ORDER, block), lambda i, info: (rows // ORDER, i))]
                if d > 0
                else [spec(2 * rows + 2 * ORDER), pl.BlockSpec((block // GROUP_CH * rows, rows), lambda i, info: (i, 0))]
            )
            + [spec(rows), spec(rows) if d > 0 else pl.BlockSpec((1, rows, block), lambda i, info: (0, 0, info[0] * per + i))]
            + [spec(ORDER + EDGE)] * chips
            + [spec(3, TAPS), spec(ORDER), spec(ORDER), spec(1), spec(1)]
            + [pl.BlockSpec(memory_space=pltpu.HBM)],
            out_specs=[whole(2 * rows, width), whole(rows, cols), whole(rows, cols)],
            scratch_shapes=[
                pltpu.VMEM((block // LANES, 2, EDGE + rows, LANES), F32),
                pltpu.VMEM((per, 2 * rows, block), BF16),
                pltpu.VMEM((cols // share, width, share), BF16),
                pltpu.SemaphoreType.DMA((cols // share,)),
            ],
        ),
        out_shape=[
            jax.ShapeDtypeStruct((2 * rows, width), BF16),
            jax.ShapeDtypeStruct((rows, cols), BF16),
            jax.ShapeDtypeStruct((rows, cols), BF16),
        ],
        compiler_params=pltpu.CompilerParams(vmem_limit_bytes=24 << 20),
        cost_estimate=BRIEF,
    )(info, *((local(prod, toep), prod) if d > 0 else (prod, toep)), *pair, *states, taps, before, wide_rates, rate_row, coef_row, weights)


def project_kernel(first, gated, weights, theirs, mine, held, sems):
    copies = weight_copies(weights, first, held, sems)
    for copy in copies:
        copy.start()
    multiply(gated[...], copies, held, theirs, mine)


def project(gated, weights, first, cols):
    rows, width = gated.shape[0] // 2, gated.shape[1]
    share = min(512, cols)
    vmem = pl.BlockSpec(memory_space=pltpu.VMEM)
    return pl.pallas_call(
        functools.partial(project_kernel, first),
        in_specs=[vmem, pl.BlockSpec(memory_space=pltpu.HBM)],
        out_specs=[vmem] * 2,
        out_shape=[jax.ShapeDtypeStruct((rows, cols), BF16)] * 2,
        scratch_shapes=[pltpu.VMEM((cols // share, width, share), BF16), pltpu.SemaphoreType.DMA((cols // share,))],
        compiler_params=pltpu.CompilerParams(vmem_limit_bytes=20 << 20),
        cost_estimate=BRIEF,
    )(gated, weights)


def finish_kernel(parts, base, *rest):
    terms, (out, ready, sems) = rest[:-3], rest[-3:]
    rows = base.shape[0]
    step = min(32, rows)
    each = len(terms) // len(parts)
    copies = []
    for i in range(rows // step):
        span = slice(i * step, (i + 1) * step)
        for p, (first, cols) in enumerate(parts):
            total = base[span, first : first + cols]
            for term in terms[p * each : (p + 1) * each]:
                total = total + term[span, :].astype(F32)
            ready[span, first : first + cols] = total.astype(BF16)
        here = pl.ds(i * step, step)
        copies.append(pltpu.make_async_copy(ready.at[here, :], out.at[here, :], sems.at[i]))
        copies[-1].start()
    for copy in copies:
        copy.wait()


def finish(parts, base, terms):
    rows, depth = base.shape
    return pl.pallas_call(
        functools.partial(finish_kernel, parts),
        in_specs=[pl.BlockSpec(memory_space=pltpu.VMEM)] * (1 + len(terms)),
        out_specs=pl.BlockSpec(memory_space=pltpu.HBM),
        out_shape=jax.ShapeDtypeStruct((rows, depth), BF16),
        scratch_shapes=[pltpu.VMEM((rows, depth), BF16), pltpu.SemaphoreType.DMA((rows // min(32, rows),))],
        compiler_params=pltpu.CompilerParams(vmem_limit_bytes=12 << 20),
        cost_estimate=BRIEF,
    )(base, *terms)


def body(chips, contexts, features, residual, short_weight, rates, residues, out_weight):
    rows, _, depth = features.shape
    width = short_weight.shape[2]
    steps = 2 * chips
    chip_rows = 2 * rows
    context_rows = steps * rows
    tp, ctx = lax.axis_index("tp"), lax.axis_index("ctx")
    chip = tp // 2
    info = tp.astype(jnp.int32).reshape(1)
    always = tp < steps

    def send(value, e):
        return lax.ppermute(value, "tp", [(i, target(i, e, chips)) for i in range(steps)])

    def send_back(value, e):
        return lax.ppermute(value, "tp", [(i, source(i, e, chips)) for i in range(steps)])

    def with_context(value, bit):
        return lax.ppermute(value, "ctx", [(i, i ^ bit) for i in range(contexts)])

    def in_hbm(value):
        return pltpu.with_memory_space_constraint(value, pltpu.HBM)

    feats = in_hbm(jnp.transpose(features, (1, 0, 2)))
    taps = in_hbm(jnp.transpose(short_weight, (1, 0, 2)))
    poles = [in_hbm(jnp.transpose(value)) for value in (rates, residues)]
    kv_out, edge0, edge1, kv_taps, rate_row, coef_row, wide_rates, *pieces = first(info, feats, taps, *poles, chips)
    tiles = width // LANES
    early = tiles // 2

    kv_taps = [kv_taps] + [send_back(kv_taps, 2 * d) for d in range(1, chips)]

    order = [(x * chips + y) * 2 for x in range(contexts) for y in range(chips)]
    edges = [
        lax.ppermute(part, ("ctx", "tp"), [(here + 1, after + c) for here, after in zip(order[:-1], order[1:])])
        for c, part in ((0, edge0), (1, edge1))
    ]

    kv_in = send(kv_out, 1)
    kv_in, edges, kv_taps, pieces = lax.optimization_barrier((kv_in, edges, kv_taps, pieces))
    pieces[:chips] = [send(piece, e) for e, piece in enumerate(pieces[:chips], 1)]

    prods, states = [None] * chips, [None] * chips
    for d in list(range(1, chips)) + [0]:
        prods[d], states[d] = front(info, d, chips, feats, kv_in, *edges, kv_taps[d])
        if d > 0:
            states[d] = send(states[d], 2 * d)
    states, prods, pieces = lax.optimization_barrier((states, prods, pieces))
    prods[1:] = [send(prods[d], 2 * d) for d in range(1, chips)]
    pieces[chips:] = [send(piece, e) for e, piece in enumerate(pieces[chips:], chips + 1)]

    def relay(states):
        by_chip = [
            sum(jnp.where((chip - d) % chips == y, state[:ORDER], 0.0) for d, state in enumerate(states))
            for y in range(chips)
        ]
        bits = [1 << i for i in range(contexts.bit_length() - 1)]
        fade = jnp.exp(-wide_rates * float(chip_rows))
        pasts = [jnp.exp(-wide_rates * float(bit * context_rows)) for bit in bits]
        places = [
            jnp.where((ctx & bit) != 0, jnp.exp(-wide_rates * ((ctx & (bit - 1)).astype(F32) * context_rows)), 0.0)
            for bit in bits
        ]
        total = by_chip[0]
        for y in range(1, chips):
            total = fade * total + by_chip[y]
        total, pasts, places = lax.optimization_barrier((total, pasts, places))
        before = jnp.zeros_like(total)
        for i, bit in enumerate(bits):
            got = with_context(total, bit)
            before = before + places[i] * got
            total = jnp.where((ctx & bit) != 0, pasts[i] * got + total, pasts[i] * total + got)
            if i == 0:
                toep = toeplitz(rate_row, coef_row, rows, 0, early)
                total, toep = lax.optimization_barrier((total, toep))
            if i == 1:
                toep = toeplitz(rate_row, coef_row, rows, early, tiles - early, toep)
                total, toep = lax.optimization_barrier((total, toep))
        return before, toep

    def no_relay(states):
        return wide_rates, jnp.zeros((width // GROUP_CH * rows, rows), BF16)

    before, toep = lax.cond(always, relay, no_relay, states)

    parts = [(0, 3 * depth // 8), (3 * depth // 8, 3 * depth // 8), (3 * depth // 4, depth // 4)]
    weights = in_hbm(out_weight)

    def gated_rows(d, prod, cols):
        return gate(
            info, d, chips, prod, toep, feats, pieces, states, taps, before, wide_rates, rate_row, coef_row,
            weights, cols,
        )

    def summed(theirs, mine):
        return mine.astype(F32) + send(theirs, 1).astype(F32)

    half = depth // 2

    def own(gated, theirs, mine):
        sums = [summed(theirs, mine), summed(*project(gated, weights, half, half))]
        return residual.astype(F32) + jnp.concatenate(sums, axis=1)

    def no_own(gated, theirs, mine):
        return jnp.zeros((rows, depth), F32)

    gateds, wholes, arriving = [], [], []
    for d in range(1, chips):
        gated, *first_part = gated_rows(d, prods[d], parts[0][1])
        gateds.append(gated)
        wholes.append(summed(*first_part).astype(BF16))
    for part in parts[1:]:

        def others(gateds, prod, part=part):
            pairs = [project(gated, weights, *part) for gated in gateds]
            came = [send(theirs, 1) for theirs, _ in pairs]
            mine = list(gated_rows(0, prod, half)) if part == parts[-1] else []
            came, mine = lax.optimization_barrier((came, mine))
            return [(own.astype(F32) + got.astype(F32)).astype(BF16) for (_, own), got in zip(pairs, came)], mine

        def no_others(gateds, prod, part=part):
            blank = [jnp.zeros((2 * rows, width), BF16)] + [jnp.zeros((rows, half), BF16)] * 2
            return [jnp.zeros((rows, part[1]), BF16) for _ in gateds], blank if part == parts[-1] else []

        gateds, wholes = lax.optimization_barrier((gateds, wholes))
        arriving.append([send_back(whole, 2 * d) for d, whole in enumerate(wholes, 1)])
        wholes, mine = lax.cond(always, others, no_others, gateds, prods[0])
    mine, wholes, arriving[0] = lax.optimization_barrier((mine, wholes, arriving[0]))
    arriving.append([send_back(whole, 2 * d) for d, whole in enumerate(wholes, 1)])
    base = lax.cond(always, own, no_own, *mine)
    return finish(parts, base, [term for terms in arriving for term in terms])


def solution(mesh):
    chips, contexts = mesh.shape["tp"] // 2, mesh.shape["ctx"]
    in_specs = (
        P(("ctx", "tp"), None, None),
        P(("ctx", "tp"), None),
        P(None, None, "tp"),
        P("tp", None),
        P("tp", None),
        P("tp", None),
    )
    return jax.shard_map(
        functools.partial(body, chips, contexts),
        mesh=mesh,
        in_specs=in_specs,
        out_specs=P(("ctx", "tp"), None),
        check_vma=False,
    )
```

```python
import functools

import jax
import jax.numpy as jnp
from jax import lax
from jax.experimental import pallas as pl
from jax.experimental.pallas import tpu as pltpu
from jax.sharding import PartitionSpec as P

ORDER = 16
GROUP_CH = 16
LANES = 128
TAPS = 7
EDGE = 8
F32 = jnp.float32
BF16 = jnp.bfloat16
PER_TILE = LANES // GROUP_CH
BRIEF = pl.CostEstimate(flops=1, bytes_accessed=1, transcendentals=0)


def halves(value):
    high = value.astype(BF16)
    return high, (value - high.astype(F32)).astype(BF16)


def dot(a, b):
    return jnp.dot(a, b, preferred_element_type=F32)


def iota(shape, dim):
    return lax.broadcasted_iota(jnp.int32, shape, dim)


def own_group():
    return iota((LANES, LANES), 0) // ORDER == iota((LANES, LANES), 1) // GROUP_CH


def target(position, e, chips):
    return 2 * ((position // 2 + e // 2) % chips) + (position % 2 + e % 2) % 2


def source(position, e, chips):
    return 2 * ((position // 2 + chips - e // 2) % chips) + (position % 2 + e % 2) % 2


def fold(product, mask):
    kept = jnp.where(mask, product, 0.0)
    return jnp.sum(kept.reshape(PER_TILE, ORDER, LANES), axis=0)


def convolve(padded, taps, start, count):
    total = taps[0:1] * padded[EDGE + start : EDGE + start + count]
    for j in range(1, TAPS):
        total = total + taps[j : j + 1] * padded[EDGE - j + start : EDGE - j + start + count]
    return total


def first_kernel(chips, info, feats, taps_in, rates_in, residues_in, kv_out, edge0, edge1, kv_taps, rate_row, coef_row, wide, *rest):
    steps = 2 * chips
    pieces, (last, taps, rates, residues, sems) = rest[: steps - 1], rest[steps - 1 :]
    rows, width = pieces[0].shape
    core = info[0] % 2
    copies = [(rates_in, rates), (residues_in, residues), (taps_in, taps), (feats.at[:, pl.ds(rows - 2 * EDGE, 2 * EDGE), :], last)]
    for j in range(chips):
        start = pl.multiple_of((2 * j + 1 - core) * width, LANES)
        for branch in range(2):
            copies.append((feats.at[branch + 1, :, pl.ds(start, width)], kv_out.at[branch, :, pl.ds(j * width, width)]))
    for e, piece in enumerate(pieces, 1):
        start = pl.multiple_of(target(info[0], e, chips) * width, LANES)
        copies.append((feats.at[0, :, pl.ds(start, width)], piece))
    copies = [pltpu.make_async_copy(*ends, sems.at[i]) for i, ends in enumerate(copies)]
    for copy in copies:
        copy.start()
    for copy in copies[:3]:
        copy.wait()

    rate, residue = rates[...], residues[...]
    coef = residue * jnp.sqrt(1.0 - jnp.exp(-2.0 * rate))
    lane_group = iota((ORDER, LANES), 1) // GROUP_CH
    diagonal = iota((ORDER, LANES), 1) % ORDER == iota((ORDER, LANES), 0)

    def spread(values, tile):
        out = jnp.broadcast_to(values[:, tile * PER_TILE : tile * PER_TILE + 1], (ORDER, LANES))
        for g in range(1, PER_TILE):
            at = tile * PER_TILE + g
            out = jnp.where(lane_group == g, jnp.broadcast_to(values[:, at : at + 1], (ORDER, LANES)), out)
        return out

    for b in range(2):
        kv_taps[b, 0:TAPS, :] = taps[b + 1]
    for tile in range(width // LANES):
        lanes = slice(tile * LANES, (tile + 1) * LANES)
        wide_rate = spread(rate, tile)
        wide[:, lanes] = wide_rate
        row = jnp.sum(jnp.where(diagonal, wide_rate, 0.0), axis=0, keepdims=True)
        rate_row[:, lanes] = row
        coef_row[:, lanes] = jnp.sum(jnp.where(diagonal, spread(coef, tile), 0.0), axis=0, keepdims=True)
        for b in range(2):
            kv_taps[b, TAPS : TAPS + 1, lanes] = row
    for copy in copies[3:]:
        copy.wait()
    for c, out in ((0, edge0), (1, edge1)):
        for j in range(chips):
            cols = slice((2 * j + c) * width, (2 * j + c + 1) * width)
            for branch in range(3):
                out[branch, :, j * width : (j + 1) * width] = last[branch, :, cols].astype(F32)[EDGE:].astype(BF16)


def first(info, feats, taps, rates, residues, chips):
    _, rows, depth = feats.shape
    width = taps.shape[2]
    others = 2 * chips - 1
    vmem = pl.BlockSpec(memory_space=pltpu.VMEM)
    return pl.pallas_call(
        functools.partial(first_kernel, chips),
        out_shape=[
            jax.ShapeDtypeStruct((2, rows, chips * width), BF16),
            jax.ShapeDtypeStruct((3, EDGE, chips * width), BF16),
            jax.ShapeDtypeStruct((3, EDGE, chips * width), BF16),
            jax.ShapeDtypeStruct((2, TAPS + 1, width), F32),
            jax.ShapeDtypeStruct((1, width), F32),
            jax.ShapeDtypeStruct((1, width), F32),
            jax.ShapeDtypeStruct((ORDER, width), F32),
        ]
        + [jax.ShapeDtypeStruct((rows, width), BF16)] * others,
        in_specs=[pl.BlockSpec(memory_space=pltpu.SMEM)] + [pl.BlockSpec(memory_space=pltpu.HBM)] * 4,
        out_specs=[vmem] * (7 + others),
        scratch_shapes=[
            pltpu.VMEM((3, 2 * EDGE, depth), BF16),
            pltpu.VMEM(taps.shape, F32),
            pltpu.VMEM(rates.shape, F32),
            pltpu.VMEM(residues.shape, F32),
            pltpu.SemaphoreType.DMA((4 + 2 * chips + others,)),
        ],
        compiler_params=pltpu.CompilerParams(vmem_limit_bytes=12 << 20),
        cost_estimate=BRIEF,
    )(info, feats, taps, rates, residues)


def front_kernel(info, k_own, v_own, kv_in, edge0, edge1, taps, prod, state, pad_k, pad_v):
    rows, width = k_own.shape[1:]
    core = info[0] % 2
    chip_rows = 2 * rows
    mine = pl.multiple_of(EDGE + core * rows, 8)
    other = pl.multiple_of(EDGE + (1 - core) * rows, 8)
    step = min(64, chip_rows)
    mask = own_group()
    age = (rows - 1 - iota((LANES, rows), 1)).astype(F32)
    for w in range(width // LANES):
        lanes = slice(w * LANES, (w + 1) * LANES)
        for b, own, pad in ((0, k_own, pad_k), (1, v_own, pad_v)):
            pad[w, 0:EDGE, :] = edge0[b + 1, :, lanes].astype(F32) + edge1[b + 1, :, lanes].astype(F32)
            pad[w, pl.ds(mine, rows), :] = own[0, :, lanes].astype(F32)
            pad[w, pl.ds(other, rows), :] = kv_in[b, :, lanes].astype(F32)
        tap_k, tap_v = taps[0, :, lanes], taps[1, :, lanes]
        for start in range(0, chip_rows, step):
            value = convolve(pad_k.at[w], tap_k, start, step) * convolve(pad_v.at[w], tap_v, start, step)
            prod[start : start + step, lanes] = value.astype(BF16)
        rate = jnp.broadcast_to(tap_k[TAPS : TAPS + 1], (LANES, LANES)).T
        high, low = halves(jnp.exp(-rate[:, :rows] * age))
        beside = jnp.concatenate([prod[0:rows, lanes], prod[rows:chip_rows, lanes]], axis=1)
        reached = dot(jnp.concatenate([high, low], axis=0), beside)
        reached = reached[:LANES] + reached[LANES:]
        inner_high, inner_low = halves(fold(reached[:, :LANES], mask))
        prod[chip_rows : chip_rows + ORDER, lanes] = inner_high
        prod[chip_rows + ORDER : chip_rows + 2 * ORDER, lanes] = inner_low
        state[0:ORDER, lanes] = fold(jnp.exp(-rate * float(rows)) * reached[:, :LANES] + reached[:, LANES:], mask)
        state[ORDER : ORDER + EDGE, lanes] = edge0[0, :, lanes].astype(F32) + edge1[0, :, lanes].astype(F32)


def front(info, d, chips, feats, kv_in, edge0, edge1, taps):
    rows = feats.shape[1]
    width = taps.shape[2]
    block = min(512, width)
    per = width // block
    stored = 2 * rows + 2 * ORDER

    def chip(info):
        return (info[0] // 2 + d) % chips

    def own(branch):
        return pl.BlockSpec((1, rows, block), lambda i, info: (branch, 0, (2 * chip(info) + info[0] % 2) * per + i))

    def of_chip(*shape):
        return pl.BlockSpec(shape + (block,), lambda i, info: (0,) * len(shape) + (chip(info) * per + i,))

    def spec(*shape):
        return pl.BlockSpec(shape + (block,), lambda i, info: (0,) * len(shape) + (i,))

    return pl.pallas_call(
        front_kernel,
        grid_spec=pltpu.PrefetchScalarGridSpec(
            num_scalar_prefetch=1,
            grid=(per,),
            in_specs=[own(1), own(2), of_chip(2, rows), of_chip(3, EDGE), of_chip(3, EDGE), spec(2, TAPS + 1)],
            out_specs=[spec(stored), spec(ORDER + EDGE)],
            scratch_shapes=[pltpu.VMEM((block // LANES, EDGE + 2 * rows, LANES), F32)] * 2,
        ),
        out_shape=[jax.ShapeDtypeStruct((stored, width), BF16), jax.ShapeDtypeStruct((ORDER + EDGE, width), F32)],
        compiler_params=pltpu.CompilerParams(vmem_limit_bytes=12 << 20),
        cost_estimate=BRIEF,
    )(info, feats, feats, kv_in, edge0, edge1, taps)


def toeplitz_kernel(chunk, rate_row, coef_row, *rest):
    out = rest[-1]
    lag = (LANES - 1 - iota((LANES, LANES), 1)).astype(F32)
    valid = iota((chunk, LANES), 1) <= iota((chunk, LANES), 0)
    for w in range(rate_row.shape[1] // LANES):
        lanes = slice(w * LANES, (w + 1) * LANES)
        rate = jnp.broadcast_to(rate_row[:, lanes], (LANES, LANES)).T
        coef = jnp.broadcast_to(coef_row[:, lanes], (LANES, LANES)).T
        taps = jnp.sum((coef * jnp.exp(-rate * lag)).reshape(PER_TILE, ORDER, LANES), axis=1)
        for g in range(PER_TILE):
            spread = jnp.broadcast_to(taps[g : g + 1], (8, LANES))
            top = pltpu.roll(spread, 1, 1, stride=1, stride_axis=0)
            block = jnp.concatenate([top] + [pltpu.roll(top, at, 1) for at in range(8, chunk, 8)], axis=0)
            at = (w * PER_TILE + g) * chunk
            out[at : at + chunk, :] = jnp.where(valid, block, 0.0)[:, :chunk].astype(BF16)


def toeplitz(rate_row, coef_row, chunk, first_tile, tiles, made=None):
    made = [] if made is None else [made]
    together = 4 if tiles % 4 == 0 and first_tile % 4 == 0 else 1
    at = first_tile // together
    return pl.pallas_call(
        functools.partial(toeplitz_kernel, chunk),
        grid=(tiles // together,),
        in_specs=[pl.BlockSpec((1, together * LANES), lambda i: (0, at + i))] * 2 + [pl.BlockSpec(memory_space=pl.ANY)] * len(made),
        out_specs=pl.BlockSpec((together * PER_TILE * chunk, chunk), lambda i: (at + i, 0)),
        out_shape=jax.ShapeDtypeStruct((rate_row.shape[1] // GROUP_CH * chunk, chunk), BF16),
        input_output_aliases={2: 0} if made else {},
        cost_estimate=BRIEF,
    )(rate_row, coef_row, *made)


def local_kernel(prod, toep, out):
    rows, width = out.shape[0] // 2, out.shape[1]
    lane_group = iota((rows, LANES), 1) // GROUP_CH
    for w in range(width // LANES):
        lanes = slice(w * LANES, (w + 1) * LANES)
        beside = jnp.concatenate([prod[:rows, lanes], prod[rows : 2 * rows, lanes]], axis=1)
        local = dot(toep[w * PER_TILE * rows : (w + 1) * PER_TILE * rows, :], beside)
        for i in range(2):
            cols = slice(i * LANES, (i + 1) * LANES)
            kept = local[:rows, cols]
            for g in range(1, PER_TILE):
                kept = jnp.where(lane_group == g, local[g * rows : (g + 1) * rows, cols], kept)
            out[i * rows : (i + 1) * rows, lanes] = kept


def local(prod, toep):
    rows, width = toep.shape[1], prod.shape[1]
    block = min(512, width)
    return pl.pallas_call(
        local_kernel,
        grid=(width // block,),
        in_specs=[
            pl.BlockSpec((prod.shape[0], block), lambda i: (0, i)),
            pl.BlockSpec((block // GROUP_CH * rows, rows), lambda i: (i, 0)),
        ],
        out_specs=pl.BlockSpec((2 * rows, block), lambda i: (0, i)),
        out_shape=jax.ShapeDtypeStruct((2 * rows, width), F32),
        compiler_params=pltpu.CompilerParams(vmem_limit_bytes=12 << 20),
        cost_estimate=BRIEF,
    )(prod, toep)


def weight_copies(weights, first, held, sems):
    share = held.shape[2]
    return [
        pltpu.make_async_copy(weights.at[:, pl.ds(first + j * share, share)], held.at[j], sems.at[j])
        for j in range(held.shape[0])
    ]


def multiply(gated, copies, held, theirs, mine):
    rows, share = theirs.shape[0], held.shape[2]
    for j, copy in enumerate(copies):
        copy.wait()
        product = dot(gated, held[j])
        theirs[:, j * share : (j + 1) * share] = product[:rows].astype(BF16)
        mine[:, j * share : (j + 1) * share] = product[rows:].astype(BF16)


def gate_kernel(d, chips, info, long_in, second, q0, q1, *rest):
    states, rest = rest[:chips], rest[chips:]
    taps, before, wide_rates, rate_row, coef_row, weights, out, theirs, mine, pad, gated, held, sems = rest
    rows, width = q0.shape[-2:]
    step = min(64, rows)
    mask = own_group()
    later = (iota((rows, LANES), 0) + 1).astype(F32)
    places = [source(info[0], 2 * d + 1, chips), source(info[0], 2 * d, chips)]
    begins = [pl.multiple_of((place % 2) * rows, rows) for place in places]
    lane_group = iota((step, LANES), 1) // GROUP_CH
    turn = pl.program_id(0)
    copies = weight_copies(weights, 0, held, sems)

    @pl.when(turn == 0)
    def _():
        for copy in copies:
            copy.start()

    for w in range(width // LANES):
        lanes = slice(w * LANES, (w + 1) * LANES)
        into_high, into_low = halves(coef_row[:, lanes] * jnp.exp(-rate_row[:, lanes] * later))
        by_chip = []
        for y in range(chips):
            value = states[0][:, lanes]
            for i in range(1, chips):
                value = jnp.where((info[0] // 2 + chips - i) % chips == y, states[i][:, lanes], value)
            by_chip.append(value)
        rate = wide_rates[:, lanes]
        fade = jnp.exp(-rate * float(2 * rows))
        state = before[:, lanes]
        for y in range(chips - 1):
            state = jnp.where(y < places[0] // 2, fade * state + by_chip[y][:ORDER], state)
        inner = (long_in[2 * rows :, lanes] if d == 0 else second[:, lanes]).astype(F32)
        halfway = inner[:ORDER] + inner[ORDER:]
        halfway = jnp.exp(-rate * float(rows)) * state + halfway
        entering = [jnp.where(place % 2 == 0, state, halfway) for place in places]
        entering = [jnp.where(mask, jnp.concatenate([value] * PER_TILE, axis=0), 0.0) for value in entering]
        state_high, state_low = halves(jnp.concatenate(entering, axis=1))
        carried = dot(into_high, state_high) + dot(into_high, state_low) + dot(into_low, state_high)
        if d == 0:
            beside = jnp.concatenate([long_in[pl.ds(at, rows), lanes] for at in begins], axis=1)
            local = dot(second[w * PER_TILE * rows : (w + 1) * PER_TILE * rows, :], beside)
        tap = taps[0, :, lanes]
        for i, (q, place) in enumerate(zip((q0, q1), places)):
            other = (q1, q0)[i]
            other = (other[0, rows - 2 * EDGE :, lanes] if d == 0 and i == 0 else other[rows - 2 * EDGE :, lanes]).astype(F32)
            pad[w, i, 0:EDGE, :] = jnp.where(place % 2 == 0, states[d][ORDER:, lanes], other[EDGE:])
            pad[w, i, EDGE:, :] = (q[0, :, lanes] if d == 0 and i == 1 else q[:, lanes]).astype(F32)
            cols_of = slice(i * LANES, (i + 1) * LANES)
            for start in range(0, rows, step):
                if d > 0:
                    long = long_in[pl.ds(begins[i] + start, step), lanes]
                else:
                    long = local[start : start + step, cols_of]
                    for g in range(1, PER_TILE):
                        at = g * rows + start
                        long = jnp.where(lane_group == g, local[at : at + step, cols_of], long)
                long = long + carried[start : start + step, cols_of]
                value = convolve(pad.at[w, i], tap, start, step) * long
                at = i * rows + start
                gated[turn, at : at + step, lanes] = value.astype(BF16)

    @pl.when(turn == pl.num_programs(0) - 1)
    def _():
        whole = jnp.concatenate([gated[i] for i in range(gated.shape[0])], axis=1)
        out[...] = whole
        multiply(whole, copies, held, theirs, mine)


def gate(info, d, chips, prod, toep, feats, pieces, states, taps, before, wide_rates, rate_row, coef_row, weights, cols):
    rows = feats.shape[1]
    width = taps.shape[2]
    block = min(512, width)
    per = width // block
    share = min(512, cols)

    def spec(*shape):
        return pl.BlockSpec(shape + (block,), lambda i, info: (0,) * len(shape) + (i,))

    def whole(*shape):
        return pl.BlockSpec(shape, lambda i, info: (0,) * len(shape))

    pair = [pieces[2 * d], pieces[2 * d - 1]] if d > 0 else [pieces[0], feats]
    return pl.pallas_call(
        functools.partial(gate_kernel, d, chips),
        grid_spec=pltpu.PrefetchScalarGridSpec(
            num_scalar_prefetch=1,
            grid=(per,),
            in_specs=(
                [spec(2 * rows), pl.BlockSpec((2 * ORDER, block), lambda i, info: (rows // ORDER, i))]
                if d > 0
                else [spec(2 * rows + 2 * ORDER), pl.BlockSpec((block // GROUP_CH * rows, rows), lambda i, info: (i, 0))]
            )
            + [spec(rows), spec(rows) if d > 0 else pl.BlockSpec((1, rows, block), lambda i, info: (0, 0, info[0] * per + i))]
            + [spec(ORDER + EDGE)] * chips
            + [spec(3, TAPS), spec(ORDER), spec(ORDER), spec(1), spec(1)]
            + [pl.BlockSpec(memory_space=pltpu.HBM)],
            out_specs=[whole(2 * rows, width), whole(rows, cols), whole(rows, cols)],
            scratch_shapes=[
                pltpu.VMEM((block // LANES, 2, EDGE + rows, LANES), F32),
                pltpu.VMEM((per, 2 * rows, block), BF16),
                pltpu.VMEM((cols // share, width, share), BF16),
                pltpu.SemaphoreType.DMA((cols // share,)),
            ],
        ),
        out_shape=[
            jax.ShapeDtypeStruct((2 * rows, width), BF16),
            jax.ShapeDtypeStruct((rows, cols), BF16),
            jax.ShapeDtypeStruct((rows, cols), BF16),
        ],
        compiler_params=pltpu.CompilerParams(vmem_limit_bytes=24 << 20),
        cost_estimate=BRIEF,
    )(info, *((local(prod, toep), prod) if d > 0 else (prod, toep)), *pair, *states, taps, before, wide_rates, rate_row, coef_row, weights)


def project_kernel(first, gated, weights, theirs, mine, held, sems):
    copies = weight_copies(weights, first, held, sems)
    for copy in copies:
        copy.start()
    multiply(gated[...], copies, held, theirs, mine)


def project(gated, weights, first, cols):
    rows, width = gated.shape[0] // 2, gated.shape[1]
    share = min(512, cols)
    vmem = pl.BlockSpec(memory_space=pltpu.VMEM)
    return pl.pallas_call(
        functools.partial(project_kernel, first),
        in_specs=[vmem, pl.BlockSpec(memory_space=pltpu.HBM)],
        out_specs=[vmem] * 2,
        out_shape=[jax.ShapeDtypeStruct((rows, cols), BF16)] * 2,
        scratch_shapes=[pltpu.VMEM((cols // share, width, share), BF16), pltpu.SemaphoreType.DMA((cols // share,))],
        compiler_params=pltpu.CompilerParams(vmem_limit_bytes=20 << 20),
        cost_estimate=BRIEF,
    )(gated, weights)


def finish_kernel(parts, base, *rest):
    terms, (out, ready, sems) = rest[:-3], rest[-3:]
    rows = base.shape[0]
    step = min(32, rows)
    each = len(terms) // len(parts)
    copies = []
    for i in range(rows // step):
        span = slice(i * step, (i + 1) * step)
        for p, (first, cols) in enumerate(parts):
            total = base[span, first : first + cols]
            for term in terms[p * each : (p + 1) * each]:
                total = total + term[span, :].astype(F32)
            ready[span, first : first + cols] = total.astype(BF16)
        here = pl.ds(i * step, step)
        copies.append(pltpu.make_async_copy(ready.at[here, :], out.at[here, :], sems.at[i]))
        copies[-1].start()
    for copy in copies:
        copy.wait()


def finish(parts, base, terms):
    rows, depth = base.shape
    return pl.pallas_call(
        functools.partial(finish_kernel, parts),
        in_specs=[pl.BlockSpec(memory_space=pltpu.VMEM)] * (1 + len(terms)),
        out_specs=pl.BlockSpec(memory_space=pltpu.HBM),
        out_shape=jax.ShapeDtypeStruct((rows, depth), BF16),
        scratch_shapes=[pltpu.VMEM((rows, depth), BF16), pltpu.SemaphoreType.DMA((rows // min(32, rows),))],
        compiler_params=pltpu.CompilerParams(vmem_limit_bytes=12 << 20),
        cost_estimate=BRIEF,
    )(base, *terms)


def body(chips, contexts, features, residual, short_weight, rates, residues, out_weight):
    rows, _, depth = features.shape
    width = short_weight.shape[2]
    steps = 2 * chips
    chip_rows = 2 * rows
    context_rows = steps * rows
    tp, ctx = lax.axis_index("tp"), lax.axis_index("ctx")
    chip = tp // 2
    info = tp.astype(jnp.int32).reshape(1)
    always = tp < steps

    def send(value, e):
        return lax.ppermute(value, "tp", [(i, target(i, e, chips)) for i in range(steps)])

    def send_back(value, e):
        return lax.ppermute(value, "tp", [(i, source(i, e, chips)) for i in range(steps)])

    def with_context(value, bit):
        return lax.ppermute(value, "ctx", [(i, i ^ bit) for i in range(contexts)])

    def in_hbm(value):
        return pltpu.with_memory_space_constraint(value, pltpu.HBM)

    feats = in_hbm(jnp.transpose(features, (1, 0, 2)))
    taps = in_hbm(jnp.transpose(short_weight, (1, 0, 2)))
    poles = [in_hbm(jnp.transpose(value)) for value in (rates, residues)]
    kv_out, edge0, edge1, kv_taps, rate_row, coef_row, wide_rates, *pieces = first(info, feats, taps, *poles, chips)
    tiles = width // LANES
    early = tiles // 2

    kv_taps = [kv_taps] + [send_back(kv_taps, 2 * d) for d in range(1, chips)]

    order = [(x * chips + y) * 2 for x in range(contexts) for y in range(chips)]
    edges = [
        lax.ppermute(part, ("ctx", "tp"), [(here + 1, after + c) for here, after in zip(order[:-1], order[1:])])
        for c, part in ((0, edge0), (1, edge1))
    ]

    kv_in = send(kv_out, 1)
    kv_in, edges, kv_taps, pieces = lax.optimization_barrier((kv_in, edges, kv_taps, pieces))
    pieces[:chips] = [send(piece, e) for e, piece in enumerate(pieces[:chips], 1)]

    prods, states = [None] * chips, [None] * chips
    for d in list(range(1, chips)) + [0]:
        prods[d], states[d] = front(info, d, chips, feats, kv_in, *edges, kv_taps[d])
        if d > 0:
            states[d] = send(states[d], 2 * d)
    states, prods, pieces = lax.optimization_barrier((states, prods, pieces))
    prods[1:] = [send(prods[d], 2 * d) for d in range(1, chips)]
    pieces[chips:] = [send(piece, e) for e, piece in enumerate(pieces[chips:], chips + 1)]

    def relay(states):
        by_chip = [
            sum(jnp.where((chip - d) % chips == y, state[:ORDER], 0.0) for d, state in enumerate(states))
            for y in range(chips)
        ]
        bits = [1 << i for i in range(contexts.bit_length() - 1)]
        fade = jnp.exp(-wide_rates * float(chip_rows))
        pasts = [jnp.exp(-wide_rates * float(bit * context_rows)) for bit in bits]
        places = [
            jnp.where((ctx & bit) != 0, jnp.exp(-wide_rates * ((ctx & (bit - 1)).astype(F32) * context_rows)), 0.0)
            for bit in bits
        ]
        total = by_chip[0]
        for y in range(1, chips):
            total = fade * total + by_chip[y]
        total, pasts, places = lax.optimization_barrier((total, pasts, places))
        before = jnp.zeros_like(total)
        for i, bit in enumerate(bits):
            got = with_context(total, bit)
            before = before + places[i] * got
            total = jnp.where((ctx & bit) != 0, pasts[i] * got + total, pasts[i] * total + got)
            if i == 0:
                toep = toeplitz(rate_row, coef_row, rows, 0, early)
                total, toep = lax.optimization_barrier((total, toep))
            if i == 1:
                toep = toeplitz(rate_row, coef_row, rows, early, tiles - early, toep)
                total, toep = lax.optimization_barrier((total, toep))
        return before, toep

    def no_relay(states):
        return wide_rates, jnp.zeros((width // GROUP_CH * rows, rows), BF16)

    before, toep = lax.cond(always, relay, no_relay, states)

    parts = [(0, 3 * depth // 8), (3 * depth // 8, 3 * depth // 8), (3 * depth // 4, depth // 4)]
    weights = in_hbm(out_weight)

    def gated_rows(d, prod, cols):
        return gate(
            info, d, chips, prod, toep, feats, pieces, states, taps, before, wide_rates, rate_row, coef_row,
            weights, cols,
        )

    def summed(theirs, mine):
        return mine.astype(F32) + send(theirs, 1).astype(F32)

    def own(prod):
        half = depth // 2
        gated, *first_half = gated_rows(0, prod, half)
        sums = [summed(*first_half), summed(*project(gated, weights, half, half))]
        return residual.astype(F32) + jnp.concatenate(sums, axis=1)

    def no_own(prod):
        return jnp.zeros((rows, depth), F32)

    gateds, wholes, arriving = [], [], []
    for d in range(1, chips):
        gated, *first_part = gated_rows(d, prods[d], parts[0][1])
        gateds.append(gated)
        wholes.append(summed(*first_part).astype(BF16))
    for part in parts[1:]:

        def others(gateds, part=part):
            return [summed(*project(gated, weights, *part)).astype(BF16) for gated in gateds]

        def no_others(gateds, part=part):
            return [jnp.zeros((rows, part[1]), BF16) for _ in gateds]

        gateds, wholes = lax.optimization_barrier((gateds, wholes))
        arriving.append([send_back(whole, 2 * d) for d, whole in enumerate(wholes, 1)])
        wholes = lax.cond(always, others, no_others, gateds)
    prods[0], wholes, arriving[0] = lax.optimization_barrier((prods[0], wholes, arriving[0]))
    arriving.append([send_back(whole, 2 * d) for d, whole in enumerate(wholes, 1)])
    base = lax.cond(always, own, no_own, prods[0])
    return finish(parts, base, [term for terms in arriving for term in terms])


def solution(mesh):
    chips, contexts = mesh.shape["tp"] // 2, mesh.shape["ctx"]
    in_specs = (
        P(("ctx", "tp"), None, None),
        P(("ctx", "tp"), None),
        P(None, None, "tp"),
        P("tp", None),
        P("tp", None),
        P("tp", None),
    )
    return jax.shard_map(
        functools.partial(body, chips, contexts),
        mesh=mesh,
        in_specs=in_specs,
        out_specs=P(("ctx", "tp"), None),
        check_vma=False,
    )
```
